256 devices in a mesh: fsdp: 32 (over z, x), rep: 2 (over y_lo), tp: 4 (over y_hi, core).
Axes of the slice: x: 4, y: 4 (y_hi: 2, y_lo: 2; y = y_hi * 2 + y_lo), z: 8, core: 2. Of those that a mesh axis runs over, the one named last changes fastest.
Arguments:
- states: bfloat16 [4, 256, 5120], P(None, ('fsdp', 'rep')), may hold values from -6 to 6
- attn_gain: bfloat16 [5120], replicated, may hold values from 0.099609375 to 1.8984375
- w_qkv: float32 [5120, 5120], P('fsdp', ('rep', 'tp')), may hold values from -0.078125 to 0.078125
- w_out: float32 [4096, 5120], P(('rep', 'tp'), 'fsdp'), may hold values from -0.09375 to 0.09375
- q_gain: float32 [128], replicated, may hold values from 1 to 4
- k_gain: float32 [128], replicated, may hold values from 0.1 to 1.9
- k_cache: bfloat16 [256, 4, 2048, 128], P(('fsdp', 'rep'), 'tp'), may hold values from -110 to 110
- v_cache: bfloat16 [256, 4, 2048, 128], P(('fsdp', 'rep'), 'tp'), may hold values from -6 to 6
- lengths: int32 [256], P(('fsdp', 'rep')), may hold values from 1024 to 2048, as said below
Outputs:
- branch: bfloat16 [4, 256, 5120], P(None, ('fsdp', 'rep'))
The draws below stay inside these ranges and needn't reach their ends.
Inputs may be any that keep to these rules, and one draw needn't show every extreme that they name: Sequence b holds cached positions 0 to lengths[b] - 1; its new token of step t stands at position lengths[b] + t.
All inputs are finite; a program needn't handle non-finite values.
Results may differ from the reference program's by a relative error of at most 0.015.
The reference program's roundings to bfloat16 on the way count: a program that leaves them out, or rounds other values in their place, can miss the bound.
Values may be sent and summed in bfloat16 or wider, within the bound.
A program may use at most 128 MiB of HBM per device.

```python
import math
import jax
import jax.numpy as jnp
from jax import lax

D = 5120
HQ = 32
HK = 4
HD = 128
CACHE = 2048
STEPS = 4
G = 8
SEQS = 256


def draw_k_cache(key, part):
    key = jax.random.fold_in(key, 11)
    shape = (SEQS, HK, CACHE, HD)
    return jnp.clip(jax.random.normal(key, shape, jnp.float32), -6.0, 6.0).astype(jnp.bfloat16)


def draw_lengths(key, part):
    key = jax.random.fold_in(key, 7)
    drawn = jax.random.randint(key, (SEQS,), CACHE // 2, CACHE + 1)
    return drawn.at[0].set(CACHE).at[1].set(CACHE // 2)


def block_levels(rng, dims, cuts, least, high):
    def one(dim, blocks):
        steps = jax.random.uniform(jax.random.fold_in(jax.random.fold_in(rng, 6), dim), (blocks,), jnp.float32, least / len(cuts), high / len(cuts))
        return jnp.repeat(jnp.exp(steps), dims[dim] // blocks).reshape((-1,) + (1,) * (len(dims) - dim - 1))

    loudness = one(*cuts[0])
    for cut in cuts[1:]:
        loudness = loudness * one(*cut)
    return loudness


def bell_draw(stream_key, shape, scale, reach, cuts=(), held_as=jnp.bfloat16):
    values = scale * jax.random.normal(stream_key, shape, jnp.float32)
    if cuts:
        values = values * block_levels(stream_key, shape, cuts, -0.22, 0.18)
    return jnp.clip(values, -reach, reach).astype(held_as)


def setup_inputs(seed: int = 0) -> dict:
    arg_keys = jax.random.split(jax.random.key(seed), 10)
    return {
        "states": bell_draw(arg_keys[0], (STEPS, SEQS, D), 1.0, 6.0, ((1, 64),)),
        "attn_gain": jnp.clip(1.0 + 0.18 * jax.random.normal(arg_keys[1], (D,), jnp.float32), 0.099609375, 1.8984375).astype(jnp.bfloat16),
        "w_qkv": bell_draw(arg_keys[2], (D, HK * (G + 2) * HD), D ** -0.5, 0.078125, ((0, 32), (1, 8)), jnp.float32),
        "w_out": bell_draw(arg_keys[3], (HQ * HD, D), (HQ * HD) ** -0.5, 0.09375, ((0, 8), (1, 32)), jnp.float32),
        "q_gain": jnp.clip(jnp.exp(jax.random.uniform(arg_keys[4], (HD,), jnp.float32, math.log(1.0), math.log(4.0))), 1.0, 4.0),
        "k_gain": jnp.clip(1.0 + 0.18 * jax.random.normal(arg_keys[5], (HD,), jnp.float32), 0.1, 1.9),
        "k_cache": draw_k_cache(jax.random.fold_in(arg_keys[9], 71), 0),
        "v_cache": bell_draw(arg_keys[7], (SEQS, HK, CACHE, HD), 1.0, 6.0, ((0, 64), (1, 4))),
        "lengths": draw_lengths(jax.random.fold_in(arg_keys[9], 71), 0),
    }


EPSILON = 1e-06
THETA = 1000000.0

def normalize(values, gain):
    return values * lax.rsqrt(lax.optimization_barrier(jnp.mean(values * values, axis=-1, keepdims=True)) + EPSILON) * gain

def rotate(values, cosine, sine):
    half = values.shape[-1] // 2
    lower = values[..., :half]
    upper = values[..., half:]
    return jnp.concatenate([lower * cosine - upper * sine, upper * cosine + lower * sine], axis=-1)

def angles(lengths, steps, head):
    half = head // 2
    frequency = jnp.exp(jnp.arange(half, dtype=jnp.float32) * (-math.log(THETA) / half))
    position = (lengths[None, :] + jnp.arange(steps, dtype=jnp.int32)[:, None]).astype(jnp.float32)
    angle = position[:, :, None] * frequency
    return (jnp.cos(angle), jnp.sin(angle))

def reference(states, attn_gain, w_qkv, w_out, q_gain, k_gain, k_cache, v_cache, lengths):
    weight_in = w_qkv.astype(jnp.bfloat16)
    weight_back = w_out.astype(jnp.bfloat16)
    normed = normalize(states.astype(jnp.float32), attn_gain.astype(jnp.float32)).astype(jnp.bfloat16)
    mixed = jnp.dot(normed.reshape(STEPS * SEQS, D), weight_in, preferred_element_type=jnp.float32)
    mixed = mixed.reshape(STEPS, SEQS, HK, G + 2, HD)
    cosine, sine = angles(lengths, STEPS, HD)
    queries = rotate(normalize(mixed[..., :G, :], q_gain.astype(jnp.float32)), cosine[:, :, None, None, :], sine[:, :, None, None, :]).astype(jnp.bfloat16)
    keys = rotate(normalize(mixed[..., G, :], k_gain.astype(jnp.float32)), cosine[:, :, None, :], sine[:, :, None, :]).astype(jnp.bfloat16)
    values = mixed[..., G + 1, :].astype(jnp.bfloat16)
    scale = 1.0 / math.sqrt(HD)
    cache_mask = jnp.arange(CACHE, dtype=jnp.int32)[None, :] < lengths[:, None]
    step_mask = jnp.arange(STEPS, dtype=jnp.int32)[None, :] <= jnp.arange(STEPS, dtype=jnp.int32)[:, None]
    old_valid = cache_mask[:, None, None, :]
    new_valid = step_mask[None, :, None, :]

    def one_group(group):
        query = lax.dynamic_index_in_dim(queries, group, 2, keepdims=False).astype(jnp.float32)
        key_new = lax.dynamic_index_in_dim(keys, group, 2, keepdims=False).astype(jnp.float32)
        value_new = lax.dynamic_index_in_dim(values, group, 2, keepdims=False).astype(jnp.float32)
        key_old = lax.dynamic_index_in_dim(k_cache, group, 1, keepdims=False).astype(jnp.float32)
        value_old = lax.dynamic_index_in_dim(v_cache, group, 1, keepdims=False).astype(jnp.float32)
        old_scores = jnp.einsum('tbqe,bce->btqc', query, key_old) * scale
        new_scores = jnp.einsum('tbqe,ube->btqu', query, key_new) * scale
        highest = jnp.maximum(lax.optimization_barrier(jnp.max(jnp.where(old_valid, old_scores, -1e+30), axis=-1, keepdims=True)), lax.optimization_barrier(jnp.max(jnp.where(new_valid, new_scores, -1e+30), axis=-1, keepdims=True)))
        old_exp = jnp.where(old_valid, jnp.exp(old_scores - highest), 0.0)
        new_exp = jnp.where(new_valid, jnp.exp(new_scores - highest), 0.0)
        total = lax.optimization_barrier(jnp.sum(old_exp, axis=-1, keepdims=True)) + lax.optimization_barrier(jnp.sum(new_exp, axis=-1, keepdims=True))
        old_weight = lax.optimization_barrier((old_exp / total).astype(jnp.bfloat16)).astype(jnp.float32)
        new_weight = lax.optimization_barrier((new_exp / total).astype(jnp.bfloat16)).astype(jnp.float32)
        context = jnp.einsum('btqc,bce->tbqe', old_weight, value_old)
        context = context + jnp.einsum('btqu,ube->tbqe', new_weight, value_new)
        return context.astype(jnp.bfloat16)
    contexts = lax.map(one_group, jnp.arange(HK, dtype=jnp.int32))
    contexts = jnp.transpose(contexts, (1, 2, 0, 3, 4)).reshape(STEPS * SEQS, HQ * HD)
    result = jnp.dot(contexts, weight_back, preferred_element_type=jnp.float32).astype(jnp.bfloat16)
    return result.reshape(STEPS, SEQS, D)
```

```python
import functools
import math

import jax
import jax.numpy as jnp
import numpy as np
from jax import lax
from jax.experimental import pallas as pl
from jax.experimental.pallas import tpu as pltpu
from jax.sharding import PartitionSpec as P

MESH = pl.DeviceIdType.MESH
EPSILON = 1e-06
THETA = 1000000.0
NZ, NX = 8, 4
STEPS, SEQS, ROWS = 4, 4, 16
HEAD, SLOTS = 128, 10
IN_ROWS, IN_COLS = 160, 640
OUT_ROWS, OUT_COLS = 512, 160
CACHE, EXTRA = 2048, 128
KEYS = CACHE + EXTRA
BF, F32 = jnp.bfloat16, jnp.float32
SUM_TYPE = jnp.bfloat16


def kernel(
    states, attn_gain, w_qkv, w_out, q_gain, k_gain, frequency, lengths, k_cache, v_cache, out,
    kbuf, vbuf, xs, nbuf, abuf, wbuf, obuf, cbuf, crecv, mbuf, mrecv, qs, ks, cs, tbuf, xbuf, pbuf, rbuf, fbuf, gbuf, ybuf,
    local_sem, w_send, w_recv, o_send, o_recv, a_send, a_recv, b_send, b_recv, c_send, c_recv,
    m_send, m_recv, t_send, t_recv, x_send, x_recv, r_send, r_recv, g_send, g_recv, y_send, y_recv,
):
    f, yl, tp = lax.axis_index("fsdp"), lax.axis_index("rep"), lax.axis_index("tp")
    z, x, yh, c = f // NX, f % NX, tp // 2, tp % 2

    def at(pz, px, pl_, ph, pc):
        return (pz * NX + px, pl_, ph * 2 + pc)

    def send(src, dst, ssem, rsem, device):
        return pltpu.make_async_remote_copy(
            src_ref=src, dst_ref=dst, send_sem=ssem, recv_sem=rsem, device_id=device, device_id_type=MESH
        )

    def z_peer(k):
        return at((z + k) % NZ, x, yl, yh, c)

    def flip(d):
        return (
            1 - yl if d & 1 else yl,
            1 - yh if d & 2 else yh,
            1 - c if d & 4 else c,
        )

    right, left = at(z, (x + 1) % NX, yl, yh, c), at(z, (x + NX - 1) % NX, yl, yh, c)

    k_copy = pltpu.make_async_copy(k_cache.at[:, 0], kbuf.at[:, pl.ds(0, CACHE)], local_sem.at[0])
    v_copy = pltpu.make_async_copy(v_cache.at[:, 0], vbuf.at[:, pl.ds(0, CACHE)], local_sem.at[1])
    k_copy.start()
    v_copy.start()

    barrier = pltpu.get_barrier_semaphore()
    peers = [right, left]
    peers += [z_peer(k) for k in range(1, NZ)]
    peers += [at(z, x, *flip(d)) for d in range(1, 8)]
    for peer in peers:
        pl.semaphore_signal(barrier, inc=1, device_id=peer, device_id_type=MESH)

    wbuf[pl.ds(x, 1)] = w_qkv[...].astype(BF)[None]
    for s in range(STEPS):
        xs[pl.ds(s * SEQS, SEQS), :] = states[s].astype(F32)
    values = xs[...]
    mean = jnp.mean(values * values, axis=-1, keepdims=True)
    normed = (values * lax.rsqrt(mean + EPSILON) * attn_gain[...].astype(F32)).astype(BF)
    for k in range(NZ):
        nbuf[k] = normed[:, k * IN_COLS : (k + 1) * IN_COLS]
    abuf[0, 0] = nbuf[z]

    pl.semaphore_wait(barrier, len(peers))

    w_right = send(wbuf.at[x], wbuf.at[x], w_send.at[0], w_recv.at[0], right)
    w_left = send(wbuf.at[x], wbuf.at[x], w_send.at[1], w_recv.at[1], left)
    w_right.start()
    w_left.start()
    a_copies = []
    for k in range(1, NZ):
        copy = send(nbuf.at[(z + k) % NZ], abuf.at[0, k], a_send.at[k], a_recv.at[k], z_peer(k))
        copy.start()
        a_copies.append(copy)

    obuf[pl.ds(x, 1)] = jnp.transpose(w_out[...]).astype(BF)[None]
    row = lax.broadcasted_iota(jnp.int32, (ROWS, HEAD), 0)
    lane = lax.broadcasted_iota(jnp.int32, (ROWS, HEAD), 1)
    position = row // SEQS
    for b in range(SEQS):
        position = position + jnp.where(row % SEQS == b, lengths[b], 0)
    angle = position.astype(F32) * frequency[...]
    cosine = jnp.cos(angle)
    sine = jnp.where(lane < HEAD // 2, -jnp.sin(angle), jnp.sin(angle))
    for b in range(SEQS):
        kbuf[b, pl.ds(CACHE, EXTRA), :] = jnp.zeros((EXTRA, HEAD), BF)
        vbuf[b, pl.ds(CACHE, EXTRA), :] = jnp.zeros((EXTRA, HEAD), BF)

    for copy in a_copies:
        copy.wait_recv()
    half = NZ // 2
    b_copies = [
        send(abuf.at[0, pl.ds(0, half)], abuf.at[1, pl.ds(0, half)], b_send.at[0], b_recv.at[0], at(z, x, 1 - yl, yh, c)),
        send(abuf.at[0, pl.ds(half, half)], abuf.at[1, pl.ds(half, half)], b_send.at[1], b_recv.at[1], at(z, x, 1 - yl, 1 - yh, c)),
    ]
    for copy in b_copies:
        copy.start()

    from_left, from_right = (x + NX - 1) % NX, (x + 1) % NX
    part = IN_ROWS // 2
    w_right.wait_recv()
    w_on_right = send(
        wbuf.at[from_left, pl.ds(0, part)], wbuf.at[from_left, pl.ds(0, part)], w_send.at[2], w_recv.at[2], right
    )
    w_on_right.start()
    w_left.wait_recv()
    w_on_left = send(
        wbuf.at[from_right, pl.ds(part, part)], wbuf.at[from_right, pl.ds(part, part)], w_send.at[3], w_recv.at[3], left
    )
    w_on_left.start()
    w_on_right.wait_recv()
    w_on_left.wait_recv()
    for copy in b_copies:
        copy.wait_recv()

    weights = wbuf[...].reshape(NX * IN_ROWS, IN_COLS)
    for rel in range(2):
        rows = abuf[rel].reshape(NZ * ROWS, IN_COLS)
        mixed = jnp.dot(rows, weights, preferred_element_type=F32)
        cbuf[:, rel] = mixed.reshape(NZ, ROWS, IN_COLS).astype(SUM_TYPE)
    c_copies = []
    for k in range(1, NZ):
        copy = send(cbuf.at[NZ - k], crecv.at[k], c_send.at[k], c_recv.at[k], z_peer(k))
        copy.start()
        c_copies.append(copy)
    o_right = send(obuf.at[x], obuf.at[x], o_send.at[0], o_recv.at[0], right)
    o_left = send(obuf.at[x], obuf.at[x], o_send.at[1], o_recv.at[1], left)
    o_right.start()
    o_left.start()
    total = cbuf[0].astype(F32)
    for copy in c_copies:
        copy.wait_recv()
    for k in range(1, NZ):
        total = total + crecv[k].astype(F32)
    mbuf[...] = total

    is_self = jnp.logical_and(yl == yh, yh == c)
    m_first = send(mbuf.at[0], mrecv.at[c], m_send.at[0], m_recv.at[c], at(z, x, yl, yl, yh))
    m_second = send(mbuf.at[1], mrecv.at[c], m_send.at[1], m_recv.at[c], at(z, x, 1 - yl, yl, yh))
    m_second.start()

    @pl.when(jnp.logical_not(is_self))
    def _():
        m_first.start()

    @pl.when(is_self)
    def _():
        mrecv[pl.ds(c, 1)] = mbuf[0][None]

    o_right.wait_recv()
    o_on_right = send(
        obuf.at[from_left, pl.ds(0, part)], obuf.at[from_left, pl.ds(0, part)], o_send.at[2], o_recv.at[2], right
    )
    o_on_right.start()
    o_left.wait_recv()
    o_on_left = send(
        obuf.at[from_right, pl.ds(part, part)], obuf.at[from_right, pl.ds(part, part)], o_send.at[3], o_recv.at[3], left
    )
    o_on_left.start()
    for cc in range(2):

        @pl.when(jnp.logical_not(jnp.logical_and(is_self, c == cc)))
        def _():
            send(mbuf.at[0], mrecv.at[cc], m_send.at[0], m_recv.at[cc], right).wait_recv()

    def slot(j):
        at_half = SLOTS // 2
        return mrecv[j // at_half, :, pl.ds((j % at_half) * HEAD, HEAD)]

    def roped(v, gain):
        n = v * lax.rsqrt(jnp.mean(v * v, axis=-1, keepdims=True) + EPSILON) * gain
        return (n * cosine + pltpu.roll(n, HEAD // 2, 1) * sine).astype(BF).astype(F32)

    for j in range(SLOTS - 2):
        qs[pl.ds(j * ROWS, ROWS), :] = roped(slot(j), q_gain[...])
    ks[pl.ds(0, ROWS), :] = roped(slot(SLOTS - 2), k_gain[...])
    ks[pl.ds(ROWS, ROWS), :] = slot(SLOTS - 1)
    k_copy.wait()
    v_copy.wait()
    queries_of = STEPS * (SLOTS - 2)
    scale = 1.0 / math.sqrt(HEAD)
    column = lax.broadcasted_iota(jnp.int32, (queries_of, KEYS), 1)
    step = lax.broadcasted_iota(jnp.int32, (queries_of, KEYS), 0) % STEPS
    new_valid = jnp.logical_and(column >= CACHE, column - CACHE <= step)
    for b in range(SEQS):
        query = qs[pl.ds(b, queries_of, stride=SEQS), :].astype(BF)
        empty = jnp.zeros((ROWS - STEPS, HEAD), F32)
        kbuf[b, pl.ds(CACHE, ROWS), :] = jnp.concatenate([ks[pl.ds(b, STEPS, stride=SEQS), :], empty], axis=0).astype(BF)
        vbuf[b, pl.ds(CACHE, ROWS), :] = jnp.concatenate([ks[pl.ds(ROWS + b, STEPS, stride=SEQS), :], empty], axis=0).astype(BF)
        scores = lax.dot_general(query, kbuf[b], (((1,), (1,)), ((), ())), preferred_element_type=F32) * scale
        valid = jnp.logical_or(column < lengths[b], new_valid)
        highest = jnp.max(jnp.where(valid, scores, -1e30), axis=-1, keepdims=True)
        exps = jnp.where(valid, jnp.exp(scores - highest), 0.0)
        probs = (exps / jnp.sum(exps, axis=-1, keepdims=True)).astype(BF)
        cs[pl.ds(b, queries_of, stride=SEQS), :] = jnp.dot(probs, vbuf[b], preferred_element_type=F32)
    per_half = (SLOTS - 2) // 2
    for j in range(SLOTS - 2):
        tbuf[j // per_half, :, pl.ds((j % per_half) * HEAD, HEAD)] = cs[pl.ds(j * ROWS, ROWS), :].astype(BF)

    for cc in range(2):
        copy = send(tbuf.at[cc], xbuf.at[0, yl], t_send.at[cc], t_recv.at[yl], at(z, x, yh, c, cc))
        own = jnp.logical_and(is_self, c == cc)

        @pl.when(jnp.logical_not(own))
        def _():
            copy.start()

        @pl.when(own)
        def _():
            xbuf[0, pl.ds(yl, 1)] = tbuf[cc][None]

    for rr in range(2):

        @pl.when(jnp.logical_not(jnp.logical_and(is_self, yl == rr)))
        def _():
            send(tbuf.at[0], xbuf.at[0, rr], t_send.at[0], t_recv.at[rr], right).wait_recv()

    x_copies = []
    for k in range(1, NZ):
        copy = send(xbuf.at[0], xbuf.at[k], x_send.at[k], x_recv.at[k], z_peer(k))
        copy.start()
        x_copies.append(copy)
    o_on_right.wait_recv()
    o_on_left.wait_recv()
    for copy in x_copies:
        copy.wait_recv()
    contexts = xbuf[...].reshape(NZ * 2 * ROWS, OUT_ROWS)
    partial = lax.dot_general(
        contexts, obuf[...].reshape(NX * OUT_COLS, OUT_ROWS), (((1,), (1,)), ((), ())), preferred_element_type=F32
    )
    pbuf[...] = partial.reshape(NZ, 2, ROWS, NX * OUT_COLS).astype(BF)

    def ahead(pl_, ph, pc):
        return ph * 2 + pl_ + pc * 4

    r_copies = []
    for d in range(1, 8):
        peer = flip(d)
        copy = send(pbuf.at[(NZ - ahead(*peer)) % NZ], rbuf.at[d], r_send.at[d], r_recv.at[d], at(z, x, *peer))
        copy.start()
        r_copies.append(copy)
    mine = ahead(yl, yh, c)
    total = pbuf[(NZ - mine) % NZ].astype(F32)
    for copy in r_copies:
        copy.wait_recv()
    for d in range(1, 8):
        total = total + rbuf[d].astype(F32)
    fbuf[...] = total.astype(BF)

    g_copy = send(fbuf, gbuf, g_send.at[0], g_recv.at[0], at((z + mine) % NZ, x, yl, yh, c))

    @pl.when(mine != 0)
    def _():
        g_copy.start()
        g_copy.wait_recv()

    @pl.when(mine == 0)
    def _():
        gbuf[...] = fbuf[...]

    block = (z + NZ - mine) % NZ
    y_copies = []
    for d in range(1, 8):
        peer = flip(d)
        copy = send(gbuf.at[peer[0]], ybuf.at[block], y_send.at[d], y_recv.at[d], at(z, x, *peer))
        copy.start()
        y_copies.append(copy)
    ybuf[pl.ds(block, 1)] = gbuf[yl][None]
    for d in range(1, 8):
        theirs = (z + NZ - ahead(*flip(d))) % NZ
        send(gbuf.at[0], ybuf.at[theirs], y_send.at[d], y_recv.at[d], right).wait_recv()
    for k in range(NZ):
        block_rows = ybuf[k].astype(F32)
        for s in range(STEPS):
            out[s, :, pl.ds(k * IN_COLS, IN_COLS)] = block_rows[s * SEQS : (s + 1) * SEQS].astype(BF)

    for copy in [w_right, w_left, w_on_right, w_on_left, o_right, o_left, o_on_right, o_on_left, m_second]:
        copy.wait_send()
    for copy in a_copies + b_copies + c_copies + x_copies + r_copies + y_copies:
        copy.wait_send()

    @pl.when(jnp.logical_not(is_self))
    def _():
        m_first.wait_send()

    for cc in range(2):

        @pl.when(jnp.logical_not(jnp.logical_and(is_self, c == cc)))
        def _():
            send(tbuf.at[cc], xbuf.at[0, 0], t_send.at[cc], t_recv.at[0], right).wait_send()

    @pl.when(mine != 0)
    def _():
        g_copy.wait_send()


def body(states, attn_gain, w_qkv, w_out, q_gain, k_gain, k_cache, v_cache, lengths):
    half = HEAD // 2
    exponent = np.arange(half, dtype=np.float64) * (-math.log(THETA) / half)
    frequency = np.tile(np.exp(exponent).astype(np.float32), 2)[None]
    width = states.shape[2]
    vmem, hbm = pl.BlockSpec(memory_space=pltpu.VMEM), pl.BlockSpec(memory_space=pl.ANY)
    dma = pltpu.SemaphoreType.DMA
    return pl.pallas_call(
        kernel,
        out_shape=jax.ShapeDtypeStruct(states.shape, BF),
        in_specs=[vmem] * 7 + [pl.BlockSpec(memory_space=pltpu.SMEM), hbm, hbm],
        out_specs=vmem,
        scratch_shapes=[
            pltpu.VMEM((SEQS, KEYS, HEAD), BF),
            pltpu.VMEM((SEQS, KEYS, HEAD), BF),
            pltpu.VMEM((ROWS, width), F32),
            pltpu.VMEM((NZ, ROWS, IN_COLS), BF),
            pltpu.VMEM((2, NZ, ROWS, IN_COLS), BF),
            pltpu.VMEM((NX, IN_ROWS, IN_COLS), BF),
            pltpu.VMEM((NX, OUT_COLS, OUT_ROWS), BF),
            pltpu.VMEM((NZ, 2, ROWS, IN_COLS), SUM_TYPE),
            pltpu.VMEM((NZ, 2, ROWS, IN_COLS), SUM_TYPE),
            pltpu.VMEM((2, ROWS, IN_COLS), F32),
            pltpu.VMEM((2, ROWS, IN_COLS), F32),
            pltpu.VMEM(((SLOTS - 2) * ROWS, HEAD), F32),
            pltpu.VMEM((2 * ROWS, HEAD), F32),
            pltpu.VMEM(((SLOTS - 2) * ROWS, HEAD), F32),
            pltpu.VMEM((2, ROWS, OUT_ROWS), BF),
            pltpu.VMEM((NZ, 2, ROWS, OUT_ROWS), BF),
            pltpu.VMEM((NZ, 2, ROWS, IN_COLS), BF),
            pltpu.VMEM((NZ, 2, ROWS, IN_COLS), BF),
            pltpu.VMEM((2, ROWS, IN_COLS), BF),
            pltpu.VMEM((2, ROWS, IN_COLS), BF),
            pltpu.VMEM((NZ, ROWS, IN_COLS), BF),
            dma((2,)),
            dma((4,)), dma((4,)),
            dma((4,)), dma((4,)),
            dma((NZ,)), dma((NZ,)),
            dma((2,)), dma((2,)),
            dma((NZ,)), dma((NZ,)),
            dma((2,)), dma((2,)),
            dma((2,)), dma((2,)),
            dma((NZ,)), dma((NZ,)),
            dma((8,)), dma((8,)),
            dma((1,)), dma((1,)),
            dma((8,)), dma((8,)),
        ],
        compiler_params=pltpu.CompilerParams(collective_id=0, has_side_effects=True, vmem_limit_bytes=48 * 1024 * 1024),
    )(
        states, attn_gain[None], w_qkv, w_out, q_gain[None], k_gain[None], jnp.asarray(frequency), lengths,
        k_cache, v_cache,
    )


def solution(mesh):
    in_specs = (
        P(None, ("fsdp", "rep"), None),
        P(),
        P("fsdp", ("rep", "tp")),
        P(("rep", "tp"), "fsdp"),
        P(),
        P(),
        P(("fsdp", "rep"), "tp", None, None),
        P(("fsdp", "rep"), "tp", None, None),
        P(("fsdp", "rep")),
    )
    out_specs = P(None, ("fsdp", "rep"), None)
    return jax.shard_map(body, mesh=mesh, in_specs=in_specs, out_specs=out_specs, check_vma=False)
```

```python
import functools
import math

import jax
import jax.numpy as jnp
import numpy as np
from jax import lax
from jax.experimental import pallas as pl
from jax.experimental.pallas import tpu as pltpu
from jax.sharding import PartitionSpec as P

MESH = pl.DeviceIdType.MESH
EPSILON = 1e-06
THETA = 1000000.0
NZ, NX = 8, 4
STEPS, SEQS, ROWS = 4, 4, 16
HEAD, SLOTS = 128, 10
IN_ROWS, IN_COLS = 160, 640
OUT_ROWS, OUT_COLS = 512, 160
CACHE, EXTRA = 2048, 128
KEYS = CACHE + EXTRA
BF, F32 = jnp.bfloat16, jnp.float32
O_AFTER = 5
O_PARTS = ((0, 80), (80, 80))
OUT_GROUPS = ((0, 4), (4, 4))
SUM_TYPE = jnp.bfloat16


def kernel(
    states_in, attn_gain_in, w_qkv_in, w_out_in, q_gain_in, k_gain_in, frequency_in, lengths_in, k_cache, v_cache, out,
    states, attn_gain, w_qkv, w_out, q_gain, k_gain, frequency, lengths,
    kbuf, vbuf, xs, nbuf, abuf, wbuf, obuf, cbuf, crecv, mrecv, qs, ks, cs, tbuf, xbuf, pbuf, precv, sbuf, rbuf, hbuf, ybuf,
    local_sem, w_send, w_recv, o_send, o_recv, a_send, a_recv, f_send, f_recv, c_send, c_recv,
    x_send, x_recv, p_send, p_recv, r_send, r_recv, h_send, h_recv,
):
    f, yl, tp = lax.axis_index("fsdp"), lax.axis_index("rep"), lax.axis_index("tp")
    z, x, yh, c = f // NX, f % NX, tp // 2, tp % 2
    y = yh * 2 + yl
    parity = z % 2
    toward = 1 - 2 * parity
    is_self = jnp.logical_and(yl == yh, yh == c)

    def at(pz, px, pl_, ph, pc):
        return (pz % NZ * NX + px % NX, pl_, ph * 2 + pc)

    def flip(d):
        return (1 - yl if d & 1 else yl, 1 - yh if d & 2 else yh, 1 - c if d & 4 else c)

    def send(src, dst, ssem, rsem, device):
        return pltpu.make_async_remote_copy(
            src_ref=src, dst_ref=dst, send_sem=ssem, recv_sem=rsem, device_id=device, device_id_type=MESH
        )

    other_core = at(z, x, yl, yh, 1 - c)
    sent = []

    def start(copy, when=None):
        sent.append((copy, when))
        if when is None:
            copy.start()
        else:
            pl.when(when)(copy.start)

    def wait(dst, rsem, when=None):
        arrival = send(dst, dst, h_send.at[0], rsem, other_core)
        if when is None:
            arrival.wait_recv()
        else:
            pl.when(when)(arrival.wait_recv)

    def finish():
        for copy, when in sent:
            if when is None:
                copy.wait_send()
            else:
                pl.when(when)(copy.wait_send)

    local = [
        (w_qkv_in, w_qkv),
        (states_in, states),
        (attn_gain_in, attn_gain),
        (lengths_in, lengths),
        (frequency_in, frequency),
        (w_out_in, w_out),
        (q_gain_in, q_gain),
        (k_gain_in, k_gain),
        (k_cache.at[:, 0], kbuf.at[:, pl.ds(0, CACHE)]),
        (v_cache.at[:, 0], vbuf.at[:, pl.ds(0, CACHE)]),
    ]
    local = [pltpu.make_async_copy(src, dst, local_sem.at[i]) for i, (src, dst) in enumerate(local)]
    for copy in local:
        copy.start()
    w_in, s_in, a_in, l_in, f_in, o_in, q_in, kg_in, k_copy, v_copy = local

    barrier = pltpu.get_barrier_semaphore()
    peers = [at(z, x + i, yl, yh, c) for i in range(1, NX)]
    peers += [at(z, x, *flip(d)) for d in range(1, 8)]
    peers += [at(z + c + 2 * i, x, 1 - yl, yh, c) for i in range(NZ // 2)]
    peers += [at(z + c + 2 * i, x, yl, yh, c) for i in range(1, NZ // 2)]
    peers += [at(z - m * toward + NZ, x, yl, yh, c) for m in range(1, 4)]
    for peer in peers:
        pl.semaphore_signal(barrier, inc=1, device_id=peer, device_id_type=MESH)

    @pl.when(c == 1)
    def _():
        pl.semaphore_signal(barrier, inc=1, device_id=at(z + 1, x, yl, yh, c), device_id_type=MESH)

    w_in.wait()
    wbuf[pl.ds(x, 1)] = w_qkv[...].astype(BF)[None]
    pl.semaphore_wait(barrier, len(peers) + c)

    right, left = at(z, x + 1, yl, yh, c), at(z, x + 3, yl, yh, c)
    rightward = ((0, 48), (48, 32), (80, 80))
    leftward = ((80, 48), (128, 32), (0, 80))

    def w_part(block, rows):
        return wbuf.at[block, pl.ds(*rows)]

    for n in range(3):
        start(send(w_part(x, rightward[n]), w_part(x, rightward[n]), w_send.at[0, n], w_recv.at[0, n], right))
        start(send(w_part(x, leftward[n]), w_part(x, leftward[n]), w_send.at[1, n], w_recv.at[1, n], left))

    s_in.wait()
    for s in range(STEPS):
        xs[pl.ds(s * SEQS, SEQS), :] = states[s].astype(F32)
    values = xs[...]
    mean = jnp.mean(values * values, axis=-1, keepdims=True)
    a_in.wait()
    normed = (values * lax.rsqrt(mean + EPSILON) * attn_gain[...].reshape(1, NZ * IN_COLS).astype(F32)).astype(BF)
    for k in range(NZ):
        nbuf[k] = normed[:, k * IN_COLS : (k + 1) * IN_COLS]

    @pl.when(c == 0)
    def _():
        abuf[0, pl.ds(yl, 1)] = nbuf[pl.ds(z, 1)]

    o_in.wait()
    obuf[0] = w_out[...].astype(BF)

    for i in (2, 1, 3, 0):
        k = c + 2 * i
        for rel in (0, 1):
            copy = send(
                nbuf.at[(z + k) % NZ], abuf.at[k, yl], a_send.at[i, rel], a_recv.at[i, rel],
                at(z + k, x, 1 - yl if rel else yl, yh, c),
            )
            start(copy, c == 1 if (i, rel) == (0, 0) else None)
    for copy in (l_in, f_in, q_in, kg_in):
        copy.wait()
    row = lax.broadcasted_iota(jnp.int32, (ROWS, HEAD), 0)
    lane = lax.broadcasted_iota(jnp.int32, (ROWS, HEAD), 1)
    position = row // SEQS
    for b in range(SEQS):
        position = position + jnp.where(row % SEQS == b, lengths[b], 0)
    angle = position.astype(F32) * frequency[...]
    cosine = jnp.cos(angle)
    sine = jnp.where(lane < HEAD // 2, -jnp.sin(angle), jnp.sin(angle))
    for b in range(SEQS):
        kbuf[b, pl.ds(CACHE, EXTRA), :] = jnp.zeros((EXTRA, HEAD), BF)
        vbuf[b, pl.ds(CACHE, EXTRA), :] = jnp.zeros((EXTRA, HEAD), BF)

    x_left, x_right, x_far = (x + 3) % NX, (x + 1) % NX, (x + 2) % NX

    def w_on(n):
        wait(w_part(x_left, rightward[n]), w_recv.at[0, n])
        start(send(w_part(x_left, rightward[n]), w_part(x_left, rightward[n]), w_send.at[2, n], w_recv.at[2, n], right))
        wait(w_part(x_right, leftward[n]), w_recv.at[1, n])
        start(send(w_part(x_right, leftward[n]), w_part(x_right, leftward[n]), w_send.at[3, n], w_recv.at[3, n], left))

    def send_back(n):
        rows = pl.ds(*O_PARTS[n])
        for m, ahead in ((3, -3), (2, 2), (1, -1)):
            target = at(z + ahead * toward + NZ, x, yl, yh, c)
            start(send(obuf.at[0, rows], obuf.at[m, rows], o_send.at[m, n], o_recv.at[m, n], target))

    w_on(0)
    for i in (0, 1, 3, 2):
        if i == 1:
            w_on(1)
        k = c + 2 * i
        for rel in (0, 1):
            wait(abuf.at[k, 1 - yl if rel else yl], a_recv.at[i, rel], c == 1 if (i, rel) == (0, 0) else None)
        start(send(abuf.at[k], abuf.at[k], f_send.at[i], f_recv.at[i], other_core))
    send_back(0)
    for i in range(NZ // 2):
        wait(abuf.at[1 - c + 2 * i], f_recv.at[i])
    wait(w_part(x_left, rightward[2]), w_recv.at[0, 2])
    wait(w_part(x_right, leftward[2]), w_recv.at[1, 2])
    for n in range(2):
        wait(w_part(x_far, rightward[n]), w_recv.at[2, n])
        wait(w_part(x_far, leftward[n]), w_recv.at[3, n])

    weights = wbuf[...].reshape(NX * IN_ROWS, IN_COLS)
    mixed = jnp.dot(abuf[...].reshape(NZ * 2 * ROWS, IN_COLS), weights, preferred_element_type=F32)
    cbuf[...] = mixed.reshape(NZ, 2, ROWS, IN_COLS).astype(SUM_TYPE)
    for k in (4, 3, 5, 2, 6, 1, 7, 0):
        for r in (0, 1):
            copy = send(cbuf.at[k, r], crecv.at[k, c], c_send.at[k, r], c_recv.at[k, c], at(z + NZ - k, x, r, yl, yh))
            start(copy, None if k else jnp.logical_not(jnp.logical_and(is_self, yl == r)))

    @pl.when(is_self)
    def _():
        crecv[0, pl.ds(c, 1)] = cbuf[0, pl.ds(yl, 1)]

    for k in (0, 1, 7, 2, 6, 3, 5, 4):
        for cc in (0, 1):
            wait(crecv.at[k, cc], c_recv.at[k, cc], None if k else jnp.logical_not(jnp.logical_and(is_self, c == cc)))
        if k == O_AFTER:
            send_back(1)
    for cc in (0, 1):
        total = crecv[0, cc].astype(F32)
        for k in range(1, NZ):
            total = total + crecv[k, cc].astype(F32)
        mrecv[cc] = total

    def slot(j):
        at_half = SLOTS // 2
        return mrecv[j // at_half, :, pl.ds((j % at_half) * HEAD, HEAD)]

    def roped(v, gain):
        n = v * lax.rsqrt(jnp.mean(v * v, axis=-1, keepdims=True) + EPSILON) * gain
        return (n * cosine + pltpu.roll(n, HEAD // 2, 1) * sine).astype(BF).astype(F32)

    for j in range(SLOTS - 2):
        qs[pl.ds(j * ROWS, ROWS), :] = roped(slot(j), q_gain[...])
    ks[pl.ds(0, ROWS), :] = roped(slot(SLOTS - 2), k_gain[...])
    ks[pl.ds(ROWS, ROWS), :] = slot(SLOTS - 1)
    k_copy.wait()
    v_copy.wait()
    queries_of = STEPS * (SLOTS - 2)
    scale = 1.0 / math.sqrt(HEAD)
    column = lax.broadcasted_iota(jnp.int32, (queries_of, KEYS), 1)
    step = lax.broadcasted_iota(jnp.int32, (queries_of, KEYS), 0) % STEPS
    new_valid = jnp.logical_and(column >= CACHE, column - CACHE <= step)
    for b in range(SEQS):
        query = qs[pl.ds(b, queries_of, stride=SEQS), :].astype(BF)
        empty = jnp.zeros((ROWS - STEPS, HEAD), F32)
        kbuf[b, pl.ds(CACHE, ROWS), :] = jnp.concatenate([ks[pl.ds(b, STEPS, stride=SEQS), :], empty], axis=0).astype(BF)
        vbuf[b, pl.ds(CACHE, ROWS), :] = jnp.concatenate([ks[pl.ds(ROWS + b, STEPS, stride=SEQS), :], empty], axis=0).astype(BF)
        scores = lax.dot_general(query, kbuf[b], (((1,), (1,)), ((), ())), preferred_element_type=F32) * scale
        valid = jnp.logical_or(column < lengths[b], new_valid)
        highest = jnp.max(jnp.where(valid, scores, -1e30), axis=-1, keepdims=True)
        exps = jnp.where(valid, jnp.exp(scores - highest), 0.0)
        probs = (exps / jnp.sum(exps, axis=-1, keepdims=True)).astype(BF)
        cs[pl.ds(b, queries_of, stride=SEQS), :] = jnp.dot(probs, vbuf[b], preferred_element_type=F32)
    per_half = (SLOTS - 2) // 2
    for j in range(SLOTS - 2):
        tbuf[j // per_half, :, pl.ds((j % per_half) * HEAD, HEAD)] = cs[pl.ds(j * ROWS, ROWS), :].astype(BF)

    order = (0, 1, 3, 4, 2, 5, 7, 6)

    def place(q, *rest):
        return at(z + q // NX * toward, x + q % NX, *rest)

    for q in reversed(order):
        back = order.index(q // NX * NX + (NX - q) % NX)
        for cc in (0, 1):
            copy = send(tbuf.at[cc], xbuf.at[back, yl], x_send.at[q, cc], x_recv.at[back, yl], place(q, yh, c, cc))
            start(copy, None if q else jnp.logical_not(jnp.logical_and(is_self, c == cc)))

    @pl.when(is_self)
    def _():
        xbuf[0, pl.ds(yl, 1)] = tbuf[pl.ds(c, 1)]

    for m in range(1, 4):
        for n in range(2):
            wait(obuf.at[m, pl.ds(*O_PARTS[n])], o_recv.at[m, n])
    back_weights = obuf[...].reshape(4 * OUT_COLS, OUT_ROWS)
    own_sum = jnp.logical_and(parity == c, c == yl)

    def multiply(first, count):
        for n in range(first, first + count):
            for r in (0, 1):
                wait(xbuf.at[n, r], x_recv.at[n, r], None if n else jnp.logical_not(jnp.logical_and(is_self, yl == r)))
        rows = xbuf[pl.ds(first, count)].reshape(count * 2 * ROWS, OUT_ROWS)
        partial = lax.dot_general(rows, back_weights, (((1,), (1,)), ((), ())), preferred_element_type=F32)
        pbuf[pl.ds(first, count)] = partial.reshape(count, 2, ROWS, 4 * OUT_COLS)
        for n in range(first, first + count):
            start(send(pbuf.at[n, 1 - c], precv.at[n], p_send.at[n], p_recv.at[n], other_core))

    def pass_on(n):
        wait(precv.at[n], p_recv.at[n])
        sbuf[n] = (pbuf[n, c] + precv[n]).astype(BF)
        for hh in (0, 1):
            copy = send(sbuf.at[n], rbuf.at[x, y], r_send.at[n, hh], r_recv.at[x, y], place(order[n], c, hh, parity))
            start(copy, None if n else jnp.logical_not(jnp.logical_and(own_sum, yh == hh)))

    for first, count in OUT_GROUPS:
        multiply(first, count)
        for n in range(first, first + count):
            pass_on(n)

    @pl.when(own_sum)
    def _():
        rbuf[pl.ds(x, 1), pl.ds(y, 1)] = sbuf[0][None, None]

    for xx in range(NX):
        for yy in range(4):
            here = jnp.logical_and(own_sum, jnp.logical_and(x == xx, y == yy))
            wait(rbuf.at[xx, yy], r_recv.at[xx, yy], jnp.logical_not(here))
        total = rbuf[xx, 0].astype(F32)
        for yy in range(1, 4):
            total = total + rbuf[xx, yy].astype(F32)
        hbuf[pl.ds(c, 1), xx] = total.astype(BF)[None]
        start(send(hbuf.at[c, xx], hbuf.at[c, xx], h_send.at[xx], h_recv.at[xx], other_core))
    def assemble(side):
        blocks = [hbuf[pl.ds(side, 1), xx].astype(F32)[0] for xx in range(NX)]
        for m in range(4):
            wide = jnp.concatenate([block[:, m * OUT_COLS : (m + 1) * OUT_COLS] for block in blocks], axis=1)
            ybuf[pl.ds((z - parity + side + (2 * side - 1) * m + NZ) % NZ, 1)] = wide[None]

    assemble(c)
    for xx in range(NX):
        wait(hbuf.at[1 - c, xx], h_recv.at[xx])
    assemble(1 - c)
    for k in range(NZ):
        block_rows = ybuf[k]
        for s in range(STEPS):
            out[s, :, pl.ds(k * IN_COLS, IN_COLS)] = block_rows[s * SEQS : (s + 1) * SEQS].astype(BF)
    finish()


def body(states, attn_gain, w_qkv, w_out, q_gain, k_gain, k_cache, v_cache, lengths):
    half = HEAD // 2
    exponent = np.arange(half, dtype=np.float64) * (-math.log(THETA) / half)
    frequency = np.tile(np.exp(exponent).astype(np.float32), 2)[None]
    width = states.shape[2]
    vmem, hbm = pl.BlockSpec(memory_space=pltpu.VMEM), pl.BlockSpec(memory_space=pltpu.HBM)
    dma = pltpu.SemaphoreType.DMA
    return pl.pallas_call(
        kernel,
        out_shape=jax.ShapeDtypeStruct(states.shape, BF),
        in_specs=[hbm] * 10,
        out_specs=vmem,
        scratch_shapes=[
            pltpu.VMEM(states.shape, BF),
            pltpu.VMEM(attn_gain.shape, BF),
            pltpu.VMEM(w_qkv.shape, F32),
            pltpu.VMEM((OUT_COLS, OUT_ROWS), F32),
            pltpu.VMEM((1, HEAD), F32),
            pltpu.VMEM((1, HEAD), F32),
            pltpu.VMEM((1, HEAD), F32),
            pltpu.SMEM((SEQS,), jnp.int32),
            pltpu.VMEM((SEQS, KEYS, HEAD), BF),
            pltpu.VMEM((SEQS, KEYS, HEAD), BF),
            pltpu.VMEM((ROWS, width), F32),
            pltpu.VMEM((NZ, ROWS, IN_COLS), BF),
            pltpu.VMEM((NZ, 2, ROWS, IN_COLS), BF),
            pltpu.VMEM((NX, IN_ROWS, IN_COLS), BF),
            pltpu.VMEM((4, OUT_COLS, OUT_ROWS), BF),
            pltpu.VMEM((NZ, 2, ROWS, IN_COLS), SUM_TYPE),
            pltpu.VMEM((NZ, 2, ROWS, IN_COLS), SUM_TYPE),
            pltpu.VMEM((2, ROWS, IN_COLS), F32),
            pltpu.VMEM(((SLOTS - 2) * ROWS, HEAD), F32),
            pltpu.VMEM((2 * ROWS, HEAD), F32),
            pltpu.VMEM(((SLOTS - 2) * ROWS, HEAD), F32),
            pltpu.VMEM((2, ROWS, OUT_ROWS), BF),
            pltpu.VMEM((8, 2, ROWS, OUT_ROWS), BF),
            pltpu.VMEM((8, 2, ROWS, IN_COLS), F32),
            pltpu.VMEM((8, ROWS, IN_COLS), F32),
            pltpu.VMEM((8, ROWS, IN_COLS), BF),
            pltpu.VMEM((NX, 4, ROWS, IN_COLS), BF),
            pltpu.VMEM((2, NX, ROWS, IN_COLS), BF),
            pltpu.VMEM((NZ, ROWS, IN_COLS), F32),
            dma((10,)),
            dma((4, 3)), dma((4, 3)),
            dma((4, 2)), dma((4, 2)),
            dma((4, 2)), dma((4, 2)),
            dma((4,)), dma((4,)),
            dma((NZ, 2)), dma((NZ, 2)),
            dma((8, 2)), dma((8, 2)),
            dma((8,)), dma((8,)),
            dma((8, 2)), dma((NX, 4)),
            dma((NX,)), dma((NX,)),
        ],
        compiler_params=pltpu.CompilerParams(collective_id=0, has_side_effects=True, vmem_limit_bytes=63 * 1024 * 1024),
    )(
        states, attn_gain, w_qkv, w_out.T, q_gain[None], k_gain[None], jnp.asarray(frequency), lengths,
        k_cache, v_cache,
    )


def solution(mesh):
    in_specs = (
        P(None, ("fsdp", "rep"), None),
        P(),
        P("fsdp", ("rep", "tp")),
        P(("rep", "tp"), "fsdp"),
        P(),
        P(),
        P(("fsdp", "rep"), "tp", None, None),
        P(("fsdp", "rep"), "tp", None, None),
        P(("fsdp", "rep")),
    )
    out_specs = P(None, ("fsdp", "rep"), None)
    return jax.shard_map(body, mesh=mesh, in_specs=in_specs, out_specs=out_specs, check_vma=False)
```

```python
import functools
import math

import jax
import jax.numpy as jnp
import numpy as np
from jax import lax
from jax.experimental import pallas as pl
from jax.experimental.pallas import tpu as pltpu
from jax.sharding import PartitionSpec as P

MESH = pl.DeviceIdType.MESH
EPSILON = 1e-06
THETA = 1000000.0
NZ, NX = 8, 4
STEPS, SEQS, ROWS = 4, 4, 16
HEAD, SLOTS = 128, 10
IN_ROWS, IN_COLS = 160, 640
OUT_ROWS, OUT_COLS = 512, 160
CACHE, EXTRA = 2048, 128
KEYS = CACHE + EXTRA
BF, F32 = jnp.bfloat16, jnp.float32
O_AFTER = 5
O_FIRST, O_SECOND = 0, 0
OUT_GROUPS = ((0, 4), (4, 4))
SUM_TYPE = jnp.bfloat16


def kernel(
    states_in, attn_gain_in, w_qkv_in, w_out_in, q_gain_in, k_gain_in, frequency_in, lengths_in, k_cache, v_cache, out,
    states, attn_gain, w_qkv, w_out, q_gain, k_gain, frequency, lengths,
    kbuf, vbuf, xs, nbuf, abuf, wbuf, obuf, cbuf, crecv, mrecv, qs, ks, cs, tbuf, xbuf, sbuf, rbuf, hbuf, ybuf,
    local_sem, w_send, w_recv, o_send, o_recv, a_send, a_recv, f_send, f_recv, c_send, c_recv,
    x_send, x_recv, q_send, q_recv, r_send, r_recv, h_send, h_recv,
):
    f, yl, tp = lax.axis_index("fsdp"), lax.axis_index("rep"), lax.axis_index("tp")
    z, x, yh, c = f // NX, f % NX, tp // 2, tp % 2
    y = yh * 2 + yl
    parity = z % 2
    toward = 1 - 2 * parity
    is_self = jnp.logical_and(yl == yh, yh == c)

    def at(pz, px, pl_, ph, pc):
        return (pz % NZ * NX + px % NX, pl_, ph * 2 + pc)

    def flip(d):
        return (1 - yl if d & 1 else yl, 1 - yh if d & 2 else yh, 1 - c if d & 4 else c)

    def send(src, dst, ssem, rsem, device):
        return pltpu.make_async_remote_copy(
            src_ref=src, dst_ref=dst, send_sem=ssem, recv_sem=rsem, device_id=device, device_id_type=MESH
        )

    other_core = at(z, x, yl, yh, 1 - c)
    sent = []

    def start(copy, when=None):
        sent.append((copy, when))
        if when is None:
            copy.start()
        else:
            pl.when(when)(copy.start)

    def wait(dst, rsem, when=None):
        arrival = send(dst, dst, h_send.at[0], rsem, other_core)
        if when is None:
            arrival.wait_recv()
        else:
            pl.when(when)(arrival.wait_recv)

    def finish():
        for copy, when in sent:
            if when is None:
                copy.wait_send()
            else:
                pl.when(when)(copy.wait_send)

    barrier = pltpu.get_barrier_semaphore()
    peers = [at(z, x + i, yl, yh, c) for i in range(1, NX)]
    peers += [at(z, x, *flip(d)) for d in range(1, 8)]
    peers += [at(z + c + 2 * i, x, 1 - yl, yh, c) for i in range(NZ // 2)]
    peers += [at(z + c + 2 * i, x, yl, yh, c) for i in range(1, NZ // 2)]
    peers += [at(z - m * toward + NZ, x, yl, yh, c) for m in range(1, 3)]
    for peer in peers:
        pl.semaphore_signal(barrier, inc=1, device_id=peer, device_id_type=MESH)

    @pl.when(c == 1)
    def _():
        pl.semaphore_signal(barrier, inc=1, device_id=at(z + 1, x, yl, yh, c), device_id_type=MESH)

    local = [
        (w_qkv_in, w_qkv),
        (states_in, states),
        (attn_gain_in, attn_gain),
        (lengths_in, lengths),
        (frequency_in, frequency),
        (w_out_in, w_out),
        (q_gain_in, q_gain),
        (k_gain_in, k_gain),
        (k_cache.at[:, 0], kbuf.at[:, pl.ds(0, CACHE)]),
        (v_cache.at[:, 0], vbuf.at[:, pl.ds(0, CACHE)]),
    ]
    local = [pltpu.make_async_copy(src, dst, local_sem.at[i]) for i, (src, dst) in enumerate(local)]
    for copy in local:
        copy.start()
    w_in, s_in, a_in, l_in, f_in, o_in, q_in, kg_in, k_copy, v_copy = local

    w_in.wait()
    wbuf[pl.ds(x, 1)] = w_qkv[...].astype(BF)[None]
    s_in.wait()
    for s in range(STEPS):
        xs[pl.ds(s * SEQS, SEQS), :] = states[s].astype(F32)
    values = xs[...]
    mean = jnp.mean(values * values, axis=-1, keepdims=True)
    a_in.wait()
    normed = (values * lax.rsqrt(mean + EPSILON) * attn_gain[...].reshape(1, NZ * IN_COLS).astype(F32)).astype(BF)
    for k in range(NZ):
        nbuf[k] = normed[:, k * IN_COLS : (k + 1) * IN_COLS]

    @pl.when(c == 0)
    def _():
        abuf[0, pl.ds(yl, 1)] = nbuf[pl.ds(z, 1)]

    o_in.wait()
    obuf[pl.ds(c, 1), 0] = w_out[...].astype(BF)[None]

    pl.semaphore_wait(barrier, len(peers) + c)

    right, left = at(z, x + 1, yl, yh, c), at(z, x + 3, yl, yh, c)
    rightward = ((0, 48), (48, 32), (80, 80))
    leftward = ((80, 48), (128, 32), (0, 80))

    def w_part(block, rows):
        return wbuf.at[block, pl.ds(*rows)]

    for n in range(3):
        start(send(w_part(x, rightward[n]), w_part(x, rightward[n]), w_send.at[0, n], w_recv.at[0, n], right))
        start(send(w_part(x, leftward[n]), w_part(x, leftward[n]), w_send.at[1, n], w_recv.at[1, n], left))

    for i in (2, 1, 3, 0):
        k = c + 2 * i
        for rel in (0, 1):
            copy = send(
                nbuf.at[(z + k) % NZ], abuf.at[k, yl], a_send.at[i, rel], a_recv.at[i, rel],
                at(z + k, x, 1 - yl if rel else yl, yh, c),
            )
            start(copy, c == 1 if (i, rel) == (0, 0) else None)
    for copy in (l_in, f_in, q_in, kg_in):
        copy.wait()
    row = lax.broadcasted_iota(jnp.int32, (ROWS, HEAD), 0)
    lane = lax.broadcasted_iota(jnp.int32, (ROWS, HEAD), 1)
    position = row // SEQS
    for b in range(SEQS):
        position = position + jnp.where(row % SEQS == b, lengths[b], 0)
    angle = position.astype(F32) * frequency[...]
    cosine = jnp.cos(angle)
    sine = jnp.where(lane < HEAD // 2, -jnp.sin(angle), jnp.sin(angle))
    for b in range(SEQS):
        kbuf[b, pl.ds(CACHE, EXTRA), :] = jnp.zeros((EXTRA, HEAD), BF)
        vbuf[b, pl.ds(CACHE, EXTRA), :] = jnp.zeros((EXTRA, HEAD), BF)

    x_left, x_right, x_far = (x + 3) % NX, (x + 1) % NX, (x + 2) % NX

    def w_on(n):
        wait(w_part(x_left, rightward[n]), w_recv.at[0, n])
        start(send(w_part(x_left, rightward[n]), w_part(x_left, rightward[n]), w_send.at[2, n], w_recv.at[2, n], right))
        wait(w_part(x_right, leftward[n]), w_recv.at[1, n])
        start(send(w_part(x_right, leftward[n]), w_part(x_right, leftward[n]), w_send.at[3, n], w_recv.at[3, n], left))

    def send_back(block, slot, ahead):
        target = at(z + ahead * toward + NZ, x, yl, yh, c)
        start(send(obuf.at[c, block], obuf.at[c, slot], o_send.at[slot], o_recv.at[slot], target))

    def share_back(slot):
        start(send(obuf.at[c, slot], obuf.at[c, slot], q_send.at[slot], q_recv.at[slot], other_core))

    w_on(0)
    for n, i in enumerate((0, 1, 3, 2)):
        if n == 1:
            w_on(1)
        k = c + 2 * i
        for rel in (0, 1):
            wait(abuf.at[k, 1 - yl if rel else yl], a_recv.at[i, rel], c == 1 if (i, rel) == (0, 0) else None)
        start(send(abuf.at[k], abuf.at[k], f_send.at[i], f_recv.at[i], other_core))
        if n == O_FIRST:
            send_back(0, 1, -1)
        if n == O_SECOND:
            send_back(0, 2, 2)
    share_back(0)
    for i in range(NZ // 2):
        wait(abuf.at[1 - c + 2 * i], f_recv.at[i])
    wait(w_part(x_left, rightward[2]), w_recv.at[0, 2])
    wait(w_part(x_right, leftward[2]), w_recv.at[1, 2])
    for n in range(2):
        wait(w_part(x_far, rightward[n]), w_recv.at[2, n])
        wait(w_part(x_far, leftward[n]), w_recv.at[3, n])

    weights = wbuf[...].reshape(NX * IN_ROWS, IN_COLS)
    mixed = jnp.dot(abuf[...].reshape(NZ * 2 * ROWS, IN_COLS), weights, preferred_element_type=F32)
    cbuf[...] = mixed.reshape(NZ, 2, ROWS, IN_COLS).astype(SUM_TYPE)
    for k in (4, 3, 5, 2, 6, 1, 7, 0):
        for r in (0, 1):
            copy = send(cbuf.at[k, r], crecv.at[k, c], c_send.at[k, r], c_recv.at[k, c], at(z + NZ - k, x, r, yl, yh))
            start(copy, None if k else jnp.logical_not(jnp.logical_and(is_self, yl == r)))

    @pl.when(is_self)
    def _():
        crecv[0, pl.ds(c, 1)] = cbuf[0, pl.ds(yl, 1)]

    for k in (0, 1, 7, 2, 6, 3, 5, 4):
        for cc in (0, 1):
            wait(crecv.at[k, cc], c_recv.at[k, cc], None if k else jnp.logical_not(jnp.logical_and(is_self, c == cc)))
        if k == O_AFTER:
            wait(obuf.at[c, 1], o_recv.at[1])
            send_back(1, 3, 2)
            share_back(1)
    wait(obuf.at[c, 2], o_recv.at[2])
    share_back(2)
    for cc in (0, 1):
        total = crecv[0, cc].astype(F32)
        for k in range(1, NZ):
            total = total + crecv[k, cc].astype(F32)
        mrecv[cc] = total

    def slot(j):
        at_half = SLOTS // 2
        return mrecv[j // at_half, :, pl.ds((j % at_half) * HEAD, HEAD)]

    def roped(v, gain):
        n = v * lax.rsqrt(jnp.mean(v * v, axis=-1, keepdims=True) + EPSILON) * gain
        return (n * cosine + pltpu.roll(n, HEAD // 2, 1) * sine).astype(BF).astype(F32)

    for j in range(SLOTS - 2):
        qs[pl.ds(j * ROWS, ROWS), :] = roped(slot(j), q_gain[...])
    ks[pl.ds(0, ROWS), :] = roped(slot(SLOTS - 2), k_gain[...])
    ks[pl.ds(ROWS, ROWS), :] = slot(SLOTS - 1)
    k_copy.wait()
    v_copy.wait()
    queries_of = STEPS * (SLOTS - 2)
    scale = 1.0 / math.sqrt(HEAD)
    column = lax.broadcasted_iota(jnp.int32, (queries_of, KEYS), 1)
    step = lax.broadcasted_iota(jnp.int32, (queries_of, KEYS), 0) % STEPS
    new_valid = jnp.logical_and(column >= CACHE, column - CACHE <= step)
    for b in range(SEQS):
        query = qs[pl.ds(b, queries_of, stride=SEQS), :].astype(BF)
        empty = jnp.zeros((ROWS - STEPS, HEAD), F32)
        kbuf[b, pl.ds(CACHE, ROWS), :] = jnp.concatenate([ks[pl.ds(b, STEPS, stride=SEQS), :], empty], axis=0).astype(BF)
        vbuf[b, pl.ds(CACHE, ROWS), :] = jnp.concatenate([ks[pl.ds(ROWS + b, STEPS, stride=SEQS), :], empty], axis=0).astype(BF)
        scores = lax.dot_general(query, kbuf[b], (((1,), (1,)), ((), ())), preferred_element_type=F32) * scale
        valid = jnp.logical_or(column < lengths[b], new_valid)
        highest = jnp.max(jnp.where(valid, scores, -1e30), axis=-1, keepdims=True)
        exps = jnp.where(valid, jnp.exp(scores - highest), 0.0)
        probs = (exps / jnp.sum(exps, axis=-1, keepdims=True)).astype(BF)
        cs[pl.ds(b, queries_of, stride=SEQS), :] = jnp.dot(probs, vbuf[b], preferred_element_type=F32)
    per_half = (SLOTS - 2) // 2
    for j in range(SLOTS - 2):
        tbuf[j // per_half, :, pl.ds((j % per_half) * HEAD, HEAD)] = cs[pl.ds(j * ROWS, ROWS), :].astype(BF)

    order = (0, 1, 3, 4, 2, 5, 7, 6)

    def place(q, *rest):
        return at(z + q // NX * toward, x + q % NX, *rest)

    for q in reversed(order):
        back = order.index(q // NX * NX + (NX - q) % NX)
        copy = send(tbuf, xbuf.at[back], x_send.at[q], x_recv.at[back], place(q, yh, c, yl))
        start(copy, None if q else jnp.logical_not(is_self))

    @pl.when(is_self)
    def _():
        xbuf[0] = tbuf[...]

    wait(obuf.at[c, 3], o_recv.at[3])
    share_back(3)
    for m in range(4):
        wait(obuf.at[1 - c, m], q_recv.at[m])
    back_weights = [obuf[half].reshape(4 * OUT_COLS, OUT_ROWS) for half in (0, 1)]
    own_sum = jnp.logical_and(parity == c, c == yl)
    for first, count in OUT_GROUPS:
        for n in range(first, first + count):
            wait(xbuf.at[n], x_recv.at[n], None if n else jnp.logical_not(is_self))
        partial = sum(
            lax.dot_general(
                xbuf[pl.ds(first, count), half].reshape(count * ROWS, OUT_ROWS), back_weights[half],
                (((1,), (1,)), ((), ())), preferred_element_type=F32,
            )
            for half in (0, 1)
        )
        sbuf[pl.ds(first, count)] = partial.reshape(count, ROWS, 4 * OUT_COLS).astype(BF)
        for n in reversed(range(first, first + count)):
            for hh in (0, 1):
                copy = send(sbuf.at[n], rbuf.at[x, y], r_send.at[n, hh], r_recv.at[x, y], place(order[n], c, hh, parity))
                start(copy, None if n else jnp.logical_not(jnp.logical_and(own_sum, yh == hh)))

    @pl.when(own_sum)
    def _():
        rbuf[pl.ds(x, 1), pl.ds(y, 1)] = sbuf[0][None, None]

    for xx in range(NX):
        for yy in range(4):
            here = jnp.logical_and(own_sum, jnp.logical_and(x == xx, y == yy))
            wait(rbuf.at[xx, yy], r_recv.at[xx, yy], jnp.logical_not(here))
        total = rbuf[xx, 0].astype(F32)
        for yy in range(1, 4):
            total = total + rbuf[xx, yy].astype(F32)
        hbuf[pl.ds(c, 1), xx] = total.astype(BF)[None]
        start(send(hbuf.at[c, xx], hbuf.at[c, xx], h_send.at[xx], h_recv.at[xx], other_core))
    def assemble(side):
        blocks = [hbuf[pl.ds(side, 1), xx].astype(F32)[0] for xx in range(NX)]
        for m in range(4):
            wide = jnp.concatenate([block[:, m * OUT_COLS : (m + 1) * OUT_COLS] for block in blocks], axis=1)
            ybuf[pl.ds((z - parity + side + (2 * side - 1) * m + NZ) % NZ, 1)] = wide[None]

    assemble(c)
    for xx in range(NX):
        wait(hbuf.at[1 - c, xx], h_recv.at[xx])
    assemble(1 - c)
    for k in range(NZ):
        block_rows = ybuf[k]
        for s in range(STEPS):
            out[s, :, pl.ds(k * IN_COLS, IN_COLS)] = block_rows[s * SEQS : (s + 1) * SEQS].astype(BF)
    finish()


def body(states, attn_gain, w_qkv, w_out, q_gain, k_gain, k_cache, v_cache, lengths):
    half = HEAD // 2
    exponent = np.arange(half, dtype=np.float64) * (-math.log(THETA) / half)
    frequency = np.tile(np.exp(exponent).astype(np.float32), 2)[None]
    width = states.shape[2]
    hbm = pl.BlockSpec(memory_space=pltpu.HBM)
    dma = pltpu.SemaphoreType.DMA
    return pl.pallas_call(
        kernel,
        out_shape=pltpu.VMEM(states.shape, BF),
        in_specs=[hbm] * 10,
        scratch_shapes=[
            pltpu.VMEM(states.shape, BF),
            pltpu.VMEM(attn_gain.shape, BF),
            pltpu.VMEM(w_qkv.shape, F32),
            pltpu.VMEM((OUT_COLS, OUT_ROWS), F32),
            pltpu.VMEM((1, HEAD), F32),
            pltpu.VMEM((1, HEAD), F32),
            pltpu.VMEM((1, HEAD), F32),
            pltpu.SMEM((SEQS,), jnp.int32),
            pltpu.VMEM((SEQS, KEYS, HEAD), BF),
            pltpu.VMEM((SEQS, KEYS, HEAD), BF),
            pltpu.VMEM((ROWS, width), F32),
            pltpu.VMEM((NZ, ROWS, IN_COLS), BF),
            pltpu.VMEM((NZ, 2, ROWS, IN_COLS), BF),
            pltpu.VMEM((NX, IN_ROWS, IN_COLS), BF),
            pltpu.VMEM((2, 4, OUT_COLS, OUT_ROWS), BF),
            pltpu.VMEM((NZ, 2, ROWS, IN_COLS), SUM_TYPE),
            pltpu.VMEM((NZ, 2, ROWS, IN_COLS), SUM_TYPE),
            pltpu.VMEM((2, ROWS, IN_COLS), F32),
            pltpu.VMEM(((SLOTS - 2) * ROWS, HEAD), F32),
            pltpu.VMEM((2 * ROWS, HEAD), F32),
            pltpu.VMEM(((SLOTS - 2) * ROWS, HEAD), F32),
            pltpu.VMEM((2, ROWS, OUT_ROWS), BF),
            pltpu.VMEM((8, 2, ROWS, OUT_ROWS), BF),
            pltpu.VMEM((8, ROWS, IN_COLS), BF),
            pltpu.VMEM((NX, 4, ROWS, IN_COLS), BF),
            pltpu.VMEM((2, NX, ROWS, IN_COLS), BF),
            pltpu.VMEM((NZ, ROWS, IN_COLS), F32),
            dma((10,)),
            dma((4, 3)), dma((4, 3)),
            dma((4,)), dma((4,)),
            dma((4, 2)), dma((4, 2)),
            dma((4,)), dma((4,)),
            dma((NZ, 2)), dma((NZ, 2)),
            dma((8,)), dma((8,)),
            dma((4,)), dma((4,)),
            dma((8, 2)), dma((NX, 4)),
            dma((NX,)), dma((NX,)),
        ],
        compiler_params=pltpu.CompilerParams(collective_id=0, has_side_effects=True, vmem_limit_bytes=63 * 1024 * 1024),
    )(
        states, attn_gain, w_qkv, w_out.T, q_gain[None], k_gain[None], jnp.asarray(frequency), lengths,
        k_cache, v_cache,
    )


def solution(mesh):
    in_specs = (
        P(None, ("fsdp", "rep"), None),
        P(),
        P("fsdp", ("rep", "tp")),
        P(("rep", "tp"), "fsdp"),
        P(),
        P(),
        P(("fsdp", "rep"), "tp", None, None),
        P(("fsdp", "rep"), "tp", None, None),
        P(("fsdp", "rep")),
    )
    out_specs = P(None, ("fsdp", "rep"), None)
    return jax.shard_map(body, mesh=mesh, in_specs=in_specs, out_specs=out_specs, check_vma=False)
```

```python
import functools
import math

import jax
import jax.numpy as jnp
import numpy as np
from jax import lax
from jax.experimental import pallas as pl
from jax.experimental.pallas import tpu as pltpu
from jax.sharding import PartitionSpec as P

MESH = pl.DeviceIdType.MESH
EPSILON = 1e-06
THETA = 1000000.0
NZ, NX = 8, 4
STEPS, SEQS, ROWS = 4, 4, 16
HEAD, SLOTS = 128, 10
IN_ROWS, IN_COLS = 160, 640
OUT_ROWS, OUT_COLS = 512, 160
CACHE, EXTRA = 2048, 128
KEYS = CACHE + EXTRA
BF, F32 = jnp.bfloat16, jnp.float32
O_AFTER = 5
O_EARLY = 80
OUT_GROUPS = ((0, 4), (4, 4))
SUM_TYPE = jnp.bfloat16


def kernel(
    states_in, attn_gain_in, w_qkv_in, w_out_in, q_gain_in, k_gain_in, frequency_in, lengths_in, k_cache, v_cache, out,
    states, attn_gain, w_qkv, w_out, q_gain, k_gain, frequency, lengths,
    kbuf, vbuf, xs, nbuf, abuf, wbuf, obuf, cbuf, crecv, mrecv, qs, ks, cs, tbuf, xbuf, sbuf, rbuf, hbuf, ybuf,
    local_sem, w_send, w_recv, o_send, o_recv, a_send, a_recv, f_send, f_recv, c_send, c_recv,
    x_send, x_recv, q_send, q_recv, r_send, r_recv, h_send, h_recv,
):
    f, yl, tp = lax.axis_index("fsdp"), lax.axis_index("rep"), lax.axis_index("tp")
    z, x, yh, c = f // NX, f % NX, tp // 2, tp % 2
    y = yh * 2 + yl
    parity = z % 2
    toward = 1 - 2 * parity
    is_self = jnp.logical_and(yl == yh, yh == c)

    def at(pz, px, pl_, ph, pc):
        return (pz % NZ * NX + px % NX, pl_, ph * 2 + pc)

    def flip(d):
        return (1 - yl if d & 1 else yl, 1 - yh if d & 2 else yh, 1 - c if d & 4 else c)

    def send(src, dst, ssem, rsem, device):
        return pltpu.make_async_remote_copy(
            src_ref=src, dst_ref=dst, send_sem=ssem, recv_sem=rsem, device_id=device, device_id_type=MESH
        )

    other_core = at(z, x, yl, yh, 1 - c)
    sent = []

    def start(copy, when=None):
        sent.append((copy, when))
        if when is None:
            copy.start()
        else:
            pl.when(when)(copy.start)

    def wait(dst, rsem, when=None):
        arrival = send(dst, dst, h_send.at[0], rsem, other_core)
        if when is None:
            arrival.wait_recv()
        else:
            pl.when(when)(arrival.wait_recv)

    def finish():
        for copy, when in sent:
            if when is None:
                copy.wait_send()
            else:
                pl.when(when)(copy.wait_send)

    barrier = pltpu.get_barrier_semaphore()
    peers = [at(z, x + i, yl, yh, c) for i in range(1, NX)]
    peers += [at(z, x, *flip(d)) for d in range(1, 8)]
    peers += [at(z + c + 2 * i, x, 1 - yl, yh, c) for i in range(NZ // 2)]
    peers += [at(z + c + 2 * i, x, yl, yh, c) for i in range(1, NZ // 2)]
    peers += [at(z - m * toward + NZ, x, yl, yh, c) for m in range(1, 3)]
    for peer in peers:
        pl.semaphore_signal(barrier, inc=1, device_id=peer, device_id_type=MESH)

    @pl.when(c == 1)
    def _():
        pl.semaphore_signal(barrier, inc=1, device_id=at(z + 1, x, yl, yh, c), device_id_type=MESH)

    local = [
        (w_qkv_in, w_qkv),
        (states_in, states),
        (attn_gain_in, attn_gain),
        (lengths_in, lengths),
        (frequency_in, frequency),
        (w_out_in, w_out),
        (q_gain_in, q_gain),
        (k_gain_in, k_gain),
        (k_cache.at[:, 0], kbuf.at[:, pl.ds(0, CACHE)]),
        (v_cache.at[:, 0], vbuf.at[:, pl.ds(0, CACHE)]),
    ]
    local = [pltpu.make_async_copy(src, dst, local_sem.at[i]) for i, (src, dst) in enumerate(local)]
    for copy in local:
        copy.start()
    w_in, s_in, a_in, l_in, f_in, o_in, q_in, kg_in, k_copy, v_copy = local

    w_in.wait()
    wbuf[pl.ds(x, 1)] = w_qkv[...].astype(BF)[None]
    s_in.wait()
    for s in range(STEPS):
        xs[pl.ds(s * SEQS, SEQS), :] = states[s].astype(F32)
    values = xs[...]
    mean = jnp.mean(values * values, axis=-1, keepdims=True)
    a_in.wait()
    normed = (values * lax.rsqrt(mean + EPSILON) * attn_gain[...].reshape(1, NZ * IN_COLS).astype(F32)).astype(BF)
    for k in range(NZ):
        nbuf[k] = normed[:, k * IN_COLS : (k + 1) * IN_COLS]

    @pl.when(c == 0)
    def _():
        abuf[0, pl.ds(yl, 1)] = nbuf[pl.ds(z, 1)]

    o_in.wait()
    obuf[pl.ds(c, 1), 0] = w_out[...].astype(BF)[None]

    pl.semaphore_wait(barrier, len(peers) + c)

    right, left = at(z, x + 1, yl, yh, c), at(z, x + 3, yl, yh, c)
    rightward = ((0, 48), (48, 32), (80, 80))
    leftward = ((80, 48), (128, 32), (0, 80))

    def w_part(block, rows):
        return wbuf.at[block, pl.ds(*rows)]

    for n in range(3):
        start(send(w_part(x, rightward[n]), w_part(x, rightward[n]), w_send.at[0, n], w_recv.at[0, n], right))
        start(send(w_part(x, leftward[n]), w_part(x, leftward[n]), w_send.at[1, n], w_recv.at[1, n], left))

    for i in (2, 1, 3, 0):
        k = c + 2 * i
        for rel in (0, 1):
            copy = send(
                nbuf.at[(z + k) % NZ], abuf.at[k, yl], a_send.at[i, rel], a_recv.at[i, rel],
                at(z + k, x, 1 - yl if rel else yl, yh, c),
            )
            start(copy, c == 1 if (i, rel) == (0, 0) else None)
    for copy in (l_in, f_in, q_in, kg_in):
        copy.wait()
    row = lax.broadcasted_iota(jnp.int32, (ROWS, HEAD), 0)
    lane = lax.broadcasted_iota(jnp.int32, (ROWS, HEAD), 1)
    position = row // SEQS
    for b in range(SEQS):
        position = position + jnp.where(row % SEQS == b, lengths[b], 0)
    angle = position.astype(F32) * frequency[...]
    cosine = jnp.cos(angle)
    sine = jnp.where(lane < HEAD // 2, -jnp.sin(angle), jnp.sin(angle))
    for b in range(SEQS):
        kbuf[b, pl.ds(CACHE, EXTRA), :] = jnp.zeros((EXTRA, HEAD), BF)
        vbuf[b, pl.ds(CACHE, EXTRA), :] = jnp.zeros((EXTRA, HEAD), BF)

    x_left, x_right, x_far = (x + 3) % NX, (x + 1) % NX, (x + 2) % NX

    def w_on(n):
        wait(w_part(x_left, rightward[n]), w_recv.at[0, n])
        start(send(w_part(x_left, rightward[n]), w_part(x_left, rightward[n]), w_send.at[2, n], w_recv.at[2, n], right))
        wait(w_part(x_right, leftward[n]), w_recv.at[1, n])
        start(send(w_part(x_right, leftward[n]), w_part(x_right, leftward[n]), w_send.at[3, n], w_recv.at[3, n], left))

    early, late = pl.ds(0, O_EARLY), pl.ds(O_EARLY, OUT_COLS - O_EARLY)

    def send_back(block, slot, ahead, rows=pl.ds(0, OUT_COLS), n=None):
        target = at(z + ahead * toward + NZ, x, yl, yh, c)
        n = slot if n is None else n
        start(send(obuf.at[c, block, rows], obuf.at[c, slot, rows], o_send.at[n], o_recv.at[n], target))

    def share_back(slot):
        start(send(obuf.at[c, slot], obuf.at[c, slot], q_send.at[slot], q_recv.at[slot], other_core))

    w_on(0)
    for n, i in enumerate((0, 1, 3, 2)):
        if n == 1:
            w_on(1)
        k = c + 2 * i
        for rel in (0, 1):
            wait(abuf.at[k, 1 - yl if rel else yl], a_recv.at[i, rel], c == 1 if (i, rel) == (0, 0) else None)
        start(send(abuf.at[k], abuf.at[k], f_send.at[i], f_recv.at[i], other_core))
        if n == 0:
            send_back(0, 1, -1)
            send_back(0, 2, 2, early)
    share_back(0)
    for i in range(NZ // 2):
        wait(abuf.at[1 - c + 2 * i], f_recv.at[i])
    wait(w_part(x_left, rightward[2]), w_recv.at[0, 2])
    wait(w_part(x_right, leftward[2]), w_recv.at[1, 2])
    for n in range(2):
        wait(w_part(x_far, rightward[n]), w_recv.at[2, n])
        wait(w_part(x_far, leftward[n]), w_recv.at[3, n])

    weights = wbuf[...].reshape(NX * IN_ROWS, IN_COLS)
    for part in ((4, 3, 5, 2), (6, 1, 7, 0)):
        if 0 in part:
            rows = jnp.concatenate([abuf[pl.ds(6, 2)], abuf[pl.ds(0, 2)]], axis=0)
        else:
            rows = abuf[pl.ds(2, 4)]
        mixed = jnp.dot(rows.reshape(NZ * ROWS, IN_COLS), weights, preferred_element_type=F32)
        mixed = mixed.reshape(NZ // 2, 2, ROWS, IN_COLS).astype(SUM_TYPE)
        if 0 in part:
            cbuf[pl.ds(6, 2)] = mixed[:2]
            cbuf[pl.ds(0, 2)] = mixed[2:]
        else:
            cbuf[pl.ds(2, 4)] = mixed
        for k in part:
            for r in (0, 1):
                copy = send(cbuf.at[k, r], crecv.at[k, c], c_send.at[k, r], c_recv.at[k, c], at(z + NZ - k, x, r, yl, yh))
                start(copy, None if k else jnp.logical_not(jnp.logical_and(is_self, yl == r)))

    @pl.when(is_self)
    def _():
        crecv[0, pl.ds(c, 1)] = cbuf[0, pl.ds(yl, 1)]

    for k in (0, 1, 7, 2, 6, 3, 5, 4):
        for cc in (0, 1):
            wait(crecv.at[k, cc], c_recv.at[k, cc], None if k else jnp.logical_not(jnp.logical_and(is_self, c == cc)))
        if k == O_AFTER:
            send_back(0, 2, 2, late, 0)
            wait(obuf.at[c, 1], o_recv.at[1])
            send_back(1, 3, 2)
            share_back(1)
    for cc in (0, 1):
        total = crecv[0, cc].astype(F32)
        for k in range(1, NZ):
            total = total + crecv[k, cc].astype(F32)
        mrecv[cc] = total

    def slot(j):
        at_half = SLOTS // 2
        return mrecv[j // at_half, :, pl.ds((j % at_half) * HEAD, HEAD)]

    def roped(v, gain):
        n = v * lax.rsqrt(jnp.mean(v * v, axis=-1, keepdims=True) + EPSILON) * gain
        return (n * cosine + pltpu.roll(n, HEAD // 2, 1) * sine).astype(BF).astype(F32)

    for j in range(SLOTS - 2):
        qs[pl.ds(j * ROWS, ROWS), :] = roped(slot(j), q_gain[...])
    ks[pl.ds(0, ROWS), :] = roped(slot(SLOTS - 2), k_gain[...])
    ks[pl.ds(ROWS, ROWS), :] = slot(SLOTS - 1)
    k_copy.wait()
    v_copy.wait()
    queries_of = STEPS * (SLOTS - 2)
    scale = math.log2(math.e) / math.sqrt(HEAD)
    column = lax.broadcasted_iota(jnp.int32, (queries_of, KEYS), 1)
    step = lax.broadcasted_iota(jnp.int32, (queries_of, KEYS), 0) % STEPS
    new_valid = jnp.logical_and(column >= CACHE, column - CACHE <= step)
    for b in range(SEQS):
        query = qs[pl.ds(b, queries_of, stride=SEQS), :].astype(BF)
        empty = jnp.zeros((ROWS - STEPS, HEAD), F32)
        kbuf[b, pl.ds(CACHE, ROWS), :] = jnp.concatenate([ks[pl.ds(b, STEPS, stride=SEQS), :], empty], axis=0).astype(BF)
        vbuf[b, pl.ds(CACHE, ROWS), :] = jnp.concatenate([ks[pl.ds(ROWS + b, STEPS, stride=SEQS), :], empty], axis=0).astype(BF)
        scores = lax.dot_general(query, kbuf[b], (((1,), (1,)), ((), ())), preferred_element_type=F32)
        valid = jnp.logical_or(column < lengths[b], new_valid)
        scores = jnp.where(valid, scores, -1e30)
        exps = jnp.exp2((scores - jnp.max(scores, axis=-1, keepdims=True)) * scale)
        probs = (exps * (1.0 / jnp.sum(exps, axis=-1, keepdims=True))).astype(BF)
        cs[pl.ds(b, queries_of, stride=SEQS), :] = jnp.dot(probs, vbuf[b], preferred_element_type=F32)
    per_half = (SLOTS - 2) // 2
    for j in range(SLOTS - 2):
        tbuf[j // per_half, :, pl.ds((j % per_half) * HEAD, HEAD)] = cs[pl.ds(j * ROWS, ROWS), :].astype(BF)

    order = (0, 1, 3, 4, 2, 5, 7, 6)

    def place(q, *rest):
        return at(z + q // NX * toward, x + q % NX, *rest)

    for q in reversed(order):
        back = order.index(q // NX * NX + (NX - q) % NX)
        copy = send(tbuf, xbuf.at[back], x_send.at[q], x_recv.at[back], place(q, yh, c, yl))
        start(copy, None if q else jnp.logical_not(is_self))

    @pl.when(is_self)
    def _():
        xbuf[0] = tbuf[...]

    wait(obuf.at[c, 2, early], o_recv.at[2])
    wait(obuf.at[c, 2, late], o_recv.at[0])
    share_back(2)
    wait(obuf.at[c, 3], o_recv.at[3])
    share_back(3)
    for m in range(4):
        wait(obuf.at[1 - c, m], q_recv.at[m])
    back_weights = [obuf[half].reshape(4 * OUT_COLS, OUT_ROWS) for half in (0, 1)]
    own_sum = jnp.logical_and(parity == c, c == yl)
    for first, count in OUT_GROUPS:
        for n in range(first, first + count):
            wait(xbuf.at[n], x_recv.at[n], None if n else jnp.logical_not(is_self))
        partial = sum(
            lax.dot_general(
                xbuf[pl.ds(first, count), half].reshape(count * ROWS, OUT_ROWS), back_weights[half],
                (((1,), (1,)), ((), ())), preferred_element_type=F32,
            )
            for half in (0, 1)
        )
        sbuf[pl.ds(first, count)] = partial.reshape(count, ROWS, 4 * OUT_COLS).astype(BF)
        for n in reversed(range(first, first + count)):
            for hh in (0, 1):
                copy = send(sbuf.at[n], rbuf.at[x, y], r_send.at[n, hh], r_recv.at[x, y], place(order[n], c, hh, parity))
                start(copy, None if n else jnp.logical_not(jnp.logical_and(own_sum, yh == hh)))

    @pl.when(own_sum)
    def _():
        rbuf[pl.ds(x, 1), pl.ds(y, 1)] = sbuf[0][None, None]

    for xx in range(NX):
        for yy in range(4):
            here = jnp.logical_and(own_sum, jnp.logical_and(x == xx, y == yy))
            wait(rbuf.at[xx, yy], r_recv.at[xx, yy], jnp.logical_not(here))
        total = rbuf[xx, 0].astype(F32)
        for yy in range(1, 4):
            total = total + rbuf[xx, yy].astype(F32)
        hbuf[pl.ds(c, 1), xx] = total.astype(BF)[None]
        start(send(hbuf.at[c, xx], hbuf.at[c, xx], h_send.at[xx], h_recv.at[xx], other_core))
    def assemble(side):
        blocks = [hbuf[pl.ds(side, 1), xx].astype(F32)[0] for xx in range(NX)]
        for m in range(4):
            wide = jnp.concatenate([block[:, m * OUT_COLS : (m + 1) * OUT_COLS] for block in blocks], axis=1)
            ybuf[pl.ds((z - parity + side + (2 * side - 1) * m + NZ) % NZ, 1)] = wide[None]

    assemble(c)
    for xx in range(NX):
        wait(hbuf.at[1 - c, xx], h_recv.at[xx])
    assemble(1 - c)
    for k in range(NZ):
        block_rows = ybuf[k]
        for s in range(STEPS):
            out[s, :, pl.ds(k * IN_COLS, IN_COLS)] = block_rows[s * SEQS : (s + 1) * SEQS].astype(BF)
    finish()


def body(states, attn_gain, w_qkv, w_out, q_gain, k_gain, k_cache, v_cache, lengths):
    half = HEAD // 2
    exponent = np.arange(half, dtype=np.float64) * (-math.log(THETA) / half)
    frequency = np.tile(np.exp(exponent).astype(np.float32), 2)[None]
    width = states.shape[2]
    hbm = pl.BlockSpec(memory_space=pltpu.HBM)
    dma = pltpu.SemaphoreType.DMA
    return pl.pallas_call(
        kernel,
        out_shape=pltpu.VMEM(states.shape, BF),
        in_specs=[hbm] * 10,
        scratch_shapes=[
            pltpu.VMEM(states.shape, BF),
            pltpu.VMEM(attn_gain.shape, BF),
            pltpu.VMEM(w_qkv.shape, F32),
            pltpu.VMEM((OUT_COLS, OUT_ROWS), F32),
            pltpu.VMEM((1, HEAD), F32),
            pltpu.VMEM((1, HEAD), F32),
            pltpu.VMEM((1, HEAD), F32),
            pltpu.SMEM((SEQS,), jnp.int32),
            pltpu.VMEM((SEQS, KEYS, HEAD), BF),
            pltpu.VMEM((SEQS, KEYS, HEAD), BF),
            pltpu.VMEM((ROWS, width), F32),
            pltpu.VMEM((NZ, ROWS, IN_COLS), BF),
            pltpu.VMEM((NZ, 2, ROWS, IN_COLS), BF),
            pltpu.VMEM((NX, IN_ROWS, IN_COLS), BF),
            pltpu.VMEM((2, 4, OUT_COLS, OUT_ROWS), BF),
            pltpu.VMEM((NZ, 2, ROWS, IN_COLS), SUM_TYPE),
            pltpu.VMEM((NZ, 2, ROWS, IN_COLS), SUM_TYPE),
            pltpu.VMEM((2, ROWS, IN_COLS), F32),
            pltpu.VMEM(((SLOTS - 2) * ROWS, HEAD), F32),
            pltpu.VMEM((2 * ROWS, HEAD), F32),
            pltpu.VMEM(((SLOTS - 2) * ROWS, HEAD), F32),
            pltpu.VMEM((2, ROWS, OUT_ROWS), BF),
            pltpu.VMEM((8, 2, ROWS, OUT_ROWS), BF),
            pltpu.VMEM((8, ROWS, IN_COLS), BF),
            pltpu.VMEM((NX, 4, ROWS, IN_COLS), BF),
            pltpu.VMEM((2, NX, ROWS, IN_COLS), BF),
            pltpu.VMEM((NZ, ROWS, IN_COLS), F32),
            dma((10,)),
            dma((4, 3)), dma((4, 3)),
            dma((4,)), dma((4,)),
            dma((4, 2)), dma((4, 2)),
            dma((4,)), dma((4,)),
            dma((NZ, 2)), dma((NZ, 2)),
            dma((8,)), dma((8,)),
            dma((4,)), dma((4,)),
            dma((8, 2)), dma((NX, 4)),
            dma((NX,)), dma((NX,)),
        ],
        compiler_params=pltpu.CompilerParams(collective_id=0, has_side_effects=True, vmem_limit_bytes=63 * 1024 * 1024),
    )(
        states, attn_gain, w_qkv, w_out.T, q_gain[None], k_gain[None], jnp.asarray(frequency), lengths,
        k_cache, v_cache,
    )


def solution(mesh):
    in_specs = (
        P(None, ("fsdp", "rep"), None),
        P(),
        P("fsdp", ("rep", "tp")),
        P(("rep", "tp"), "fsdp"),
        P(),
        P(),
        P(("fsdp", "rep"), "tp", None, None),
        P(("fsdp", "rep"), "tp", None, None),
        P(("fsdp", "rep")),
    )
    out_specs = P(None, ("fsdp", "rep"), None)
    return jax.shard_map(body, mesh=mesh, in_specs=in_specs, out_specs=out_specs, check_vma=False)
```

```python
import functools
import math

import jax
import jax.numpy as jnp
import numpy as np
from jax import lax
from jax.experimental import pallas as pl
from jax.experimental.pallas import tpu as pltpu
from jax.sharding import PartitionSpec as P

MESH = pl.DeviceIdType.MESH
EPSILON = 1e-06
THETA = 1000000.0
NZ, NX = 8, 4
STEPS, SEQS, ROWS = 4, 4, 16
HEAD, SLOTS = 128, 10
IN_ROWS, IN_COLS = 160, 640
OUT_ROWS, OUT_COLS = 512, 160
CACHE, EXTRA = 2048, 128
KEYS = CACHE + EXTRA
BF, F32 = jnp.bfloat16, jnp.float32
O_AFTER = 5
O_EARLY = 80
OUT_GROUPS = ((0, 4), (4, 4))
SUM_TYPE = jnp.bfloat16


def kernel(
    states_in, attn_gain_in, w_qkv_in, w_out_in, q_gain_in, k_gain_in, frequency_in, lengths_in, k_cache, v_cache, out,
    states, attn_gain, w_qkv, w_out, q_gain, k_gain, frequency, lengths,
    kbuf, vbuf, xs, nbuf, abuf, wbuf, obuf, cbuf, crecv, mrecv, qs, ks, cs, tbuf, xbuf, sbuf, rbuf, hbuf, ybuf,
    local_sem, w_send, w_recv, o_send, o_recv, a_send, a_recv, f_send, f_recv, c_send, c_recv,
    x_send, x_recv, q_send, q_recv, r_send, r_recv, h_send, h_recv,
):
    f, yl, tp = lax.axis_index("fsdp"), lax.axis_index("rep"), lax.axis_index("tp")
    z, x, yh, c = f // NX, f % NX, tp // 2, tp % 2
    y = yh * 2 + yl
    parity = z % 2
    toward = 1 - 2 * parity
    is_self = jnp.logical_and(yl == yh, yh == c)

    def at(pz, px, pl_, ph, pc):
        return (pz % NZ * NX + px % NX, pl_, ph * 2 + pc)

    def flip(d):
        return (1 - yl if d & 1 else yl, 1 - yh if d & 2 else yh, 1 - c if d & 4 else c)

    def send(src, dst, ssem, rsem, device):
        return pltpu.make_async_remote_copy(
            src_ref=src, dst_ref=dst, send_sem=ssem, recv_sem=rsem, device_id=device, device_id_type=MESH
        )

    other_core = at(z, x, yl, yh, 1 - c)
    sent = []

    def start(copy, when=None):
        sent.append((copy, when))
        if when is None:
            copy.start()
        else:
            pl.when(when)(copy.start)

    def wait(dst, rsem, when=None):
        arrival = send(dst, dst, h_send.at[0], rsem, other_core)
        if when is None:
            arrival.wait_recv()
        else:
            pl.when(when)(arrival.wait_recv)

    def finish(keep=0):
        done = len(sent) - keep
        for copy, when in sent[:done]:
            if when is None:
                copy.wait_send()
            else:
                pl.when(when)(copy.wait_send)
        del sent[:done]

    barrier = pltpu.get_barrier_semaphore()
    peers = [at(z, x + i, yl, yh, c) for i in range(1, NX)]
    peers += [at(z, x, *flip(d)) for d in range(1, 8)]
    peers += [at(z + c + 2 * i, x, 1 - yl, yh, c) for i in range(NZ // 2)]
    peers += [at(z + c + 2 * i, x, yl, yh, c) for i in range(1, NZ // 2)]
    peers += [at(z - m * toward + NZ, x, yl, yh, c) for m in range(1, 3)]
    for peer in peers:
        pl.semaphore_signal(barrier, inc=1, device_id=peer, device_id_type=MESH)

    @pl.when(c == 1)
    def _():
        pl.semaphore_signal(barrier, inc=1, device_id=at(z + 1, x, yl, yh, c), device_id_type=MESH)

    local = [
        (w_qkv_in, w_qkv),
        (states_in, states),
        (attn_gain_in, attn_gain),
        (lengths_in, lengths),
        (frequency_in, frequency),
        (w_out_in, w_out),
        (q_gain_in, q_gain),
        (k_gain_in, k_gain),
        (k_cache.at[:, 0], kbuf.at[:, pl.ds(0, CACHE)]),
        (v_cache.at[:, 0], vbuf.at[:, pl.ds(0, CACHE)]),
    ]
    local = [pltpu.make_async_copy(src, dst, local_sem.at[i]) for i, (src, dst) in enumerate(local)]
    for copy in local[:3] + local[8:]:
        copy.start()
    w_in, s_in, a_in, l_in, f_in, o_in, q_in, kg_in, k_copy, v_copy = local

    w_in.wait()
    wbuf[pl.ds(x, 1)] = w_qkv[...].astype(BF)[None]
    s_in.wait()
    for s in range(STEPS):
        xs[pl.ds(s * SEQS, SEQS), :] = states[s].astype(F32)
    values = xs[...]
    mean = jnp.mean(values * values, axis=-1, keepdims=True)
    a_in.wait()
    normed = (values * lax.rsqrt(mean + EPSILON) * attn_gain[...].reshape(1, NZ * IN_COLS).astype(F32)).astype(BF)
    for k in range(NZ):
        nbuf[k] = normed[:, k * IN_COLS : (k + 1) * IN_COLS]

    @pl.when(c == 0)
    def _():
        abuf[0, pl.ds(yl, 1)] = nbuf[pl.ds(z, 1)]

    for copy in local[3:8]:
        copy.start()

    pl.semaphore_wait(barrier, len(peers) + c)

    right, left = at(z, x + 1, yl, yh, c), at(z, x + 3, yl, yh, c)
    rightward = ((0, 48), (48, 32), (80, 80))
    leftward = ((80, 48), (128, 32), (0, 80))

    def w_part(block, rows):
        return wbuf.at[block, pl.ds(*rows)]

    for n in range(3):
        start(send(w_part(x, rightward[n]), w_part(x, rightward[n]), w_send.at[0, n], w_recv.at[0, n], right))
        start(send(w_part(x, leftward[n]), w_part(x, leftward[n]), w_send.at[1, n], w_recv.at[1, n], left))

    for i in (2, 1, 3, 0):
        k = c + 2 * i
        for rel in (0, 1):
            copy = send(
                nbuf.at[(z + k) % NZ], abuf.at[k, yl], a_send.at[i, rel], a_recv.at[i, rel],
                at(z + k, x, 1 - yl if rel else yl, yh, c),
            )
            start(copy, c == 1 if (i, rel) == (0, 0) else None)
    o_in.wait()
    obuf[pl.ds(c, 1), 0] = w_out[...].astype(BF)[None]
    for copy in (l_in, f_in, q_in, kg_in):
        copy.wait()
    row = lax.broadcasted_iota(jnp.int32, (ROWS, HEAD), 0)
    lane = lax.broadcasted_iota(jnp.int32, (ROWS, HEAD), 1)
    position = row // SEQS
    for b in range(SEQS):
        position = position + jnp.where(row % SEQS == b, lengths[b], 0)
    angle = position.astype(F32) * frequency[...]
    cosine = jnp.cos(angle)
    sine = jnp.where(lane < HEAD // 2, -jnp.sin(angle), jnp.sin(angle))
    for b in range(SEQS):
        kbuf[b, pl.ds(CACHE, EXTRA), :] = jnp.zeros((EXTRA, HEAD), BF)
        vbuf[b, pl.ds(CACHE, EXTRA), :] = jnp.zeros((EXTRA, HEAD), BF)

    x_left, x_right, x_far = (x + 3) % NX, (x + 1) % NX, (x + 2) % NX

    def w_on(n):
        wait(w_part(x_left, rightward[n]), w_recv.at[0, n])
        start(send(w_part(x_left, rightward[n]), w_part(x_left, rightward[n]), w_send.at[2, n], w_recv.at[2, n], right))
        wait(w_part(x_right, leftward[n]), w_recv.at[1, n])
        start(send(w_part(x_right, leftward[n]), w_part(x_right, leftward[n]), w_send.at[3, n], w_recv.at[3, n], left))

    early, late = pl.ds(0, O_EARLY), pl.ds(O_EARLY, OUT_COLS - O_EARLY)

    def send_back(block, slot, ahead, rows=pl.ds(0, OUT_COLS), n=None):
        target = at(z + ahead * toward + NZ, x, yl, yh, c)
        n = slot if n is None else n
        start(send(obuf.at[c, block, rows], obuf.at[c, slot, rows], o_send.at[n], o_recv.at[n], target))

    def share_back(slot):
        start(send(obuf.at[c, slot], obuf.at[c, slot], q_send.at[slot], q_recv.at[slot], other_core))

    w_on(0)
    for n, i in enumerate((0, 1, 3, 2)):
        if n == 1:
            w_on(1)
        k = c + 2 * i
        for rel in (0, 1):
            wait(abuf.at[k, 1 - yl if rel else yl], a_recv.at[i, rel], c == 1 if (i, rel) == (0, 0) else None)
        start(send(abuf.at[k], abuf.at[k], f_send.at[i], f_recv.at[i], other_core))
        if n == 0:
            send_back(0, 1, -1)
            send_back(0, 2, 2, early)
    share_back(0)
    for i in range(NZ // 2):
        wait(abuf.at[1 - c + 2 * i], f_recv.at[i])
    wait(w_part(x_left, rightward[2]), w_recv.at[0, 2])
    wait(w_part(x_right, leftward[2]), w_recv.at[1, 2])
    for n in range(2):
        wait(w_part(x_far, rightward[n]), w_recv.at[2, n])
        wait(w_part(x_far, leftward[n]), w_recv.at[3, n])

    weights = wbuf[...].reshape(NX * IN_ROWS, IN_COLS)
    for part in ((4, 3, 5, 2), (6, 1, 7, 0)):
        if 0 in part:
            rows = jnp.concatenate([abuf[pl.ds(6, 2)], abuf[pl.ds(0, 2)]], axis=0)
        else:
            rows = abuf[pl.ds(2, 4)]
        mixed = jnp.dot(rows.reshape(NZ * ROWS, IN_COLS), weights, preferred_element_type=F32)
        mixed = mixed.reshape(NZ // 2, 2, ROWS, IN_COLS).astype(SUM_TYPE)
        if 0 in part:
            cbuf[pl.ds(6, 2)] = mixed[:2]
            cbuf[pl.ds(0, 2)] = mixed[2:]
        else:
            cbuf[pl.ds(2, 4)] = mixed
        for k in part:
            for r in (0, 1):
                copy = send(cbuf.at[k, r], crecv.at[k, c], c_send.at[k, r], c_recv.at[k, c], at(z + NZ - k, x, r, yl, yh))
                start(copy, None if k else jnp.logical_not(jnp.logical_and(is_self, yl == r)))

    @pl.when(is_self)
    def _():
        crecv[0, pl.ds(c, 1)] = cbuf[0, pl.ds(yl, 1)]

    total = [jnp.zeros((ROWS, IN_COLS), F32)] * 2
    for k in (0, 1, 7, 2, 6, 3, 5, 4):
        for cc in (0, 1):
            wait(crecv.at[k, cc], c_recv.at[k, cc], None if k else jnp.logical_not(jnp.logical_and(is_self, c == cc)))
            total[cc] = total[cc] + crecv[k, cc].astype(F32)
        if k == O_AFTER:
            send_back(0, 2, 2, late, 0)
            wait(obuf.at[c, 1], o_recv.at[1])
            send_back(1, 3, 2)
            share_back(1)
    for cc in (0, 1):
        mrecv[cc] = total[cc]

    def slot(j):
        at_half = SLOTS // 2
        return mrecv[j // at_half, :, pl.ds((j % at_half) * HEAD, HEAD)]

    def roped(v, gain):
        n = v * lax.rsqrt(jnp.mean(v * v, axis=-1, keepdims=True) + EPSILON) * gain
        return (n * cosine + pltpu.roll(n, HEAD // 2, 1) * sine).astype(BF).astype(F32)

    for j in range(SLOTS - 2):
        qs[pl.ds(j * ROWS, ROWS), :] = roped(slot(j), q_gain[...])
    ks[pl.ds(0, ROWS), :] = roped(slot(SLOTS - 2), k_gain[...])
    ks[pl.ds(ROWS, ROWS), :] = slot(SLOTS - 1)
    k_copy.wait()
    v_copy.wait()
    queries_of = STEPS * (SLOTS - 2)
    scale = math.log2(math.e) / math.sqrt(HEAD)
    column = lax.broadcasted_iota(jnp.int32, (queries_of, KEYS), 1)
    step = lax.broadcasted_iota(jnp.int32, (queries_of, KEYS), 0) % STEPS
    new_valid = jnp.logical_and(column >= CACHE, column - CACHE <= step)
    for b in range(SEQS):
        query = qs[pl.ds(b, queries_of, stride=SEQS), :].astype(BF)
        empty = jnp.zeros((ROWS - STEPS, HEAD), F32)
        kbuf[b, pl.ds(CACHE, ROWS), :] = jnp.concatenate([ks[pl.ds(b, STEPS, stride=SEQS), :], empty], axis=0).astype(BF)
        vbuf[b, pl.ds(CACHE, ROWS), :] = jnp.concatenate([ks[pl.ds(ROWS + b, STEPS, stride=SEQS), :], empty], axis=0).astype(BF)
        scores = lax.dot_general(query, kbuf[b], (((1,), (1,)), ((), ())), preferred_element_type=F32)
        valid = jnp.logical_or(column < lengths[b], new_valid)
        scores = jnp.where(valid, scores, -1e30)
        exps = jnp.exp2((scores - jnp.max(scores, axis=-1, keepdims=True)) * scale)
        probs = (exps * (1.0 / jnp.sum(exps, axis=-1, keepdims=True))).astype(BF)
        cs[pl.ds(b, queries_of, stride=SEQS), :] = jnp.dot(probs, vbuf[b], preferred_element_type=F32)
    per_half = (SLOTS - 2) // 2
    for j in range(SLOTS - 2):
        tbuf[j // per_half, :, pl.ds((j % per_half) * HEAD, HEAD)] = cs[pl.ds(j * ROWS, ROWS), :].astype(BF)

    order = (0, 1, 3, 4, 2, 5, 7, 6)

    def place(q, *rest):
        return at(z + q // NX * toward, x + q % NX, *rest)

    for q in reversed(order):
        back = order.index(q // NX * NX + (NX - q) % NX)
        copy = send(tbuf, xbuf.at[back], x_send.at[q], x_recv.at[back], place(q, yh, c, yl))
        start(copy, None if q else jnp.logical_not(is_self))

    @pl.when(is_self)
    def _():
        xbuf[0] = tbuf[...]

    finish(len(order))
    wait(obuf.at[c, 2, early], o_recv.at[2])
    wait(obuf.at[c, 2, late], o_recv.at[0])
    share_back(2)
    wait(obuf.at[c, 3], o_recv.at[3])
    share_back(3)
    for m in range(4):
        wait(obuf.at[1 - c, m], q_recv.at[m])
    back_weights = [obuf[half].reshape(4 * OUT_COLS, OUT_ROWS) for half in (0, 1)]
    own_sum = jnp.logical_and(parity == c, c == yl)
    for first, count in OUT_GROUPS:
        for n in range(first, first + count):
            wait(xbuf.at[n], x_recv.at[n], None if n else jnp.logical_not(is_self))
        partial = sum(
            lax.dot_general(
                xbuf[pl.ds(first, count), half].reshape(count * ROWS, OUT_ROWS), back_weights[half],
                (((1,), (1,)), ((), ())), preferred_element_type=F32,
            )
            for half in (0, 1)
        )
        sbuf[pl.ds(first, count)] = partial.reshape(count, ROWS, 4 * OUT_COLS).astype(BF)
        for n in reversed(range(first, first + count)):
            for hh in (0, 1):
                copy = send(sbuf.at[n], rbuf.at[x, y], r_send.at[n, hh], r_recv.at[x, y], place(order[n], c, hh, parity))
                start(copy, None if n else jnp.logical_not(jnp.logical_and(own_sum, yh == hh)))

    finish(2 * len(order))

    @pl.when(own_sum)
    def _():
        rbuf[pl.ds(x, 1), pl.ds(y, 1)] = sbuf[0][None, None]

    for xx in range(NX):
        for yy in range(4):
            here = jnp.logical_and(own_sum, jnp.logical_and(x == xx, y == yy))
            wait(rbuf.at[xx, yy], r_recv.at[xx, yy], jnp.logical_not(here))
        total = rbuf[xx, 0].astype(F32)
        for yy in range(1, 4):
            total = total + rbuf[xx, yy].astype(F32)
        hbuf[pl.ds(c, 1), xx] = total.astype(BF)[None]
        start(send(hbuf.at[c, xx], hbuf.at[c, xx], h_send.at[xx], h_recv.at[xx], other_core))
    def assemble(side):
        blocks = [hbuf[pl.ds(side, 1), xx].astype(F32)[0] for xx in range(NX)]
        for m in range(4):
            wide = jnp.concatenate([block[:, m * OUT_COLS : (m + 1) * OUT_COLS] for block in blocks], axis=1)
            ybuf[pl.ds((z - parity + side + (2 * side - 1) * m + NZ) % NZ, 1)] = wide[None]

    assemble(c)
    for xx in range(NX):
        wait(hbuf.at[1 - c, xx], h_recv.at[xx])
    assemble(1 - c)
    for k in range(NZ):
        block_rows = ybuf[k]
        for s in range(STEPS):
            out[s, :, pl.ds(k * IN_COLS, IN_COLS)] = block_rows[s * SEQS : (s + 1) * SEQS].astype(BF)
    finish()


def body(states, attn_gain, w_qkv, w_out, q_gain, k_gain, k_cache, v_cache, lengths):
    half = HEAD // 2
    exponent = np.arange(half, dtype=np.float64) * (-math.log(THETA) / half)
    frequency = np.tile(np.exp(exponent).astype(np.float32), 2)[None]
    width = states.shape[2]
    hbm = pl.BlockSpec(memory_space=pltpu.HBM)
    dma = pltpu.SemaphoreType.DMA
    return pl.pallas_call(
        kernel,
        out_shape=pltpu.VMEM(states.shape, BF),
        in_specs=[hbm] * 10,
        scratch_shapes=[
            pltpu.VMEM(states.shape, BF),
            pltpu.VMEM(attn_gain.shape, BF),
            pltpu.VMEM(w_qkv.shape, F32),
            pltpu.VMEM((OUT_COLS, OUT_ROWS), F32),
            pltpu.VMEM((1, HEAD), F32),
            pltpu.VMEM((1, HEAD), F32),
            pltpu.VMEM((1, HEAD), F32),
            pltpu.SMEM((SEQS,), jnp.int32),
            pltpu.VMEM((SEQS, KEYS, HEAD), BF),
            pltpu.VMEM((SEQS, KEYS, HEAD), BF),
            pltpu.VMEM((ROWS, width), F32),
            pltpu.VMEM((NZ, ROWS, IN_COLS), BF),
            pltpu.VMEM((NZ, 2, ROWS, IN_COLS), BF),
            pltpu.VMEM((NX, IN_ROWS, IN_COLS), BF),
            pltpu.VMEM((2, 4, OUT_COLS, OUT_ROWS), BF),
            pltpu.VMEM((NZ, 2, ROWS, IN_COLS), SUM_TYPE),
            pltpu.VMEM((NZ, 2, ROWS, IN_COLS), SUM_TYPE),
            pltpu.VMEM((2, ROWS, IN_COLS), F32),
            pltpu.VMEM(((SLOTS - 2) * ROWS, HEAD), F32),
            pltpu.VMEM((2 * ROWS, HEAD), F32),
            pltpu.VMEM(((SLOTS - 2) * ROWS, HEAD), F32),
            pltpu.VMEM((2, ROWS, OUT_ROWS), BF),
            pltpu.VMEM((8, 2, ROWS, OUT_ROWS), BF),
            pltpu.VMEM((8, ROWS, IN_COLS), BF),
            pltpu.VMEM((NX, 4, ROWS, IN_COLS), BF),
            pltpu.VMEM((2, NX, ROWS, IN_COLS), BF),
            pltpu.VMEM((NZ, ROWS, IN_COLS), F32),
            dma((10,)),
            dma((4, 3)), dma((4, 3)),
            dma((4,)), dma((4,)),
            dma((4, 2)), dma((4, 2)),
            dma((4,)), dma((4,)),
            dma((NZ, 2)), dma((NZ, 2)),
            dma((8,)), dma((8,)),
            dma((4,)), dma((4,)),
            dma((8, 2)), dma((NX, 4)),
            dma((NX,)), dma((NX,)),
        ],
        compiler_params=pltpu.CompilerParams(collective_id=0, has_side_effects=True, vmem_limit_bytes=63 * 1024 * 1024),
    )(
        states, attn_gain, w_qkv, w_out.T, q_gain[None], k_gain[None], jnp.asarray(frequency), lengths,
        k_cache, v_cache,
    )


def solution(mesh):
    in_specs = (
        P(None, ("fsdp", "rep"), None),
        P(),
        P("fsdp", ("rep", "tp")),
        P(("rep", "tp"), "fsdp"),
        P(),
        P(),
        P(("fsdp", "rep"), "tp", None, None),
        P(("fsdp", "rep"), "tp", None, None),
        P(("fsdp", "rep")),
    )
    out_specs = P(None, ("fsdp", "rep"), None)
    return jax.shard_map(body, mesh=mesh, in_specs=in_specs, out_specs=out_specs, check_vma=False)
```
